32 devices in a mesh: seq: 8 (over z, x), fsdp: 4 (over y, core).
Axes of the slice: x: 2, y: 2, z: 4, core: 2. Of those that a mesh axis runs over, the one named last changes fastest.
Arguments:
- tokens: bfloat16 [6144, 6144], P('seq'), may hold values from -30 to 30
- w_query: bfloat16 [6144, 32, 128], P('seq', 'fsdp'), may hold values from -0.078125 to 0.078125
- w_keyval: bfloat16 [6144, 32, 256], P('seq', 'fsdp'), may hold values from -40 to 40
- doc_lengths: int32 [8], replicated, may hold values from 1 to 3072, 6144 in all
- norm_gain: bfloat16 [4096], P('fsdp'), may hold values from 0.25 to 1.75
Outputs:
- attended: bfloat16 [6144, 4096], P('seq', 'fsdp')
The draws below stay inside these ranges and needn't reach their ends.
Inputs may be any that keep to these rules, and one draw needn't show every extreme that they name: `doc_lengths`: lengths are positive and sum to 6144; the longest document has exactly 3072 tokens.
All inputs are finite; a program needn't handle non-finite values.
Results may differ from the reference program's by a relative error of at most 0.0034.
Values may be sent and summed in bfloat16 or wider, within the bound.
No kernel may reach another device: no remote copies, remote signals or barrier semaphores. Data moves between devices by JAX's collectives and lax.ppermute only.
A program may use at most 128 MiB of HBM per device.

```python
import math
import jax
import jax.numpy as jnp
import numpy as np
from jax import lax

D = 6144
H = 32
DH = 128
TOK_DEV = 768
NDOCS = 8
TOKENS = 6144
N_SEQ = 8


def draw_tokens(key, part):
    first, second = jax.random.split(key)
    scales = jnp.exp(jax.random.uniform(first, (TOKENS, 1), jnp.float32, math.log(0.5), math.log(5.0)))
    entries = jnp.clip(jax.random.normal(second, (TOKENS, D), jnp.float32), -6.0, 6.0)
    return (entries * scales).astype(jnp.bfloat16)


def draw_w_keyval(key, part):
    first, second = jax.random.split(key)
    ramp = 10.0 ** (jnp.arange(H, dtype=jnp.float32) / (H - 1))
    jitter = jnp.exp(jax.random.uniform(second, (H,), jnp.float32, math.log(0.7), math.log(1.4)))
    entries = jnp.clip(jax.random.normal(first, (D, H, 2 * DH), jnp.float32), -4.0, 4.0)
    column = jnp.concatenate([jnp.ones((H, DH), jnp.float32), (ramp * jitter)[:, None] * jnp.ones((1, DH), jnp.float32)], axis=1)
    return (entries * column[None] / math.sqrt(D)).astype(jnp.bfloat16)


def levels(stream_key, dims, cuts, low, top_value):
    loudness, own = 1.0, jax.random.fold_in(stream_key, 6)
    for axis_at, parts in cuts:
        heights = jnp.exp(jax.random.uniform(jax.random.fold_in(own, axis_at), (parts,), jnp.float32, low / len(cuts), top_value / len(cuts)))
        loudness = loudness * jnp.repeat(heights, dims[axis_at] // parts).reshape([-1 if axis == axis_at else 1 for axis in range(len(dims))])
    return loudness


def split_up(amount, total, bound, lean):
    weights = [(1 << 20) // math.isqrt(grade ** lean) + 1 for grade in range(2, amount + 1)]
    rest, given = total - bound - (amount - 1), [1] * (amount - 1)
    while rest > 0:
        free = [i for i in range(amount - 1) if given[i] < bound]
        whole, remaining = sum([weights[i] for i in free]), rest
        for i in free:
            addition = min(bound - given[i], max(1, remaining * weights[i] // whole), rest)
            given[i] = given[i] + addition
            rest = rest - addition
    return np.array([bound] + given)


def ragged(stream_key, count, total, reach, slope):
    if count == 2:
        one = jax.random.randint(stream_key, (), max(1, total - reach), min(reach, total - 1) + 1)
        return jnp.stack([one, total - one])
    lengths = jnp.asarray(split_up(count, total, reach, slope), jnp.int32)
    pairs = (count - 1) // 2
    source_of, taker = lengths[1:1 + 2 * pairs:2], lengths[2:2 + 2 * pairs:2]
    slack = jnp.minimum(source_of - 1, reach - taker)
    passed = jax.random.randint(jax.random.fold_in(stream_key, 1), (pairs,), 0, 1 << 20) % (slack + 1)
    lengths = lengths.at[1:1 + 2 * pairs:2].set(source_of - passed).at[2:2 + 2 * pairs:2].set(taker + passed)
    return lengths[jax.random.permutation(jax.random.fold_in(stream_key, 2), count)]


def bell_draw(key, extent, width, reach, pieces=(), kind=jnp.bfloat16):
    result = jax.random.normal(key, extent, jnp.float32) * width
    if len(pieces) > 0:
        result = levels(key, extent, pieces, -0.22, 0.18) * result
    return jnp.clip(result, min=-reach, max=reach).astype(kind)


def setup_inputs(seed: int = 0) -> dict:
    key_list = jax.random.split(jax.random.key(seed), 6)
    return {
        "tokens": draw_tokens(jax.random.fold_in(key_list[5], 71), 0),
        "w_query": bell_draw(key_list[1], (D, H, DH), D ** -0.5, 0.078125, ((0, 8), (1, 4))),
        "w_keyval": draw_w_keyval(jax.random.fold_in(key_list[5], 71), 0),
        "doc_lengths": ragged(key_list[3], NDOCS, TOKENS, TOKENS // 2, 2).astype(jnp.int32),
        "norm_gain": jnp.clip(1.0 + 0.15 * jax.random.normal(key_list[4], (H * DH,), jnp.float32), 0.25, 1.75).astype(jnp.bfloat16),
    }


def doc_index(positions, doc_ends):
    return lax.optimization_barrier(jnp.sum((positions[:, None] >= doc_ends[None, :]).astype(jnp.int32), axis=1)).astype(jnp.int32)

def reference(tokens, w_query, w_keyval, doc_lengths, norm_gain):
    high = lax.Precision.HIGHEST
    doc_ends = jnp.cumsum(doc_lengths).astype(jnp.int32)
    query_matrix = w_query.reshape(D, H * DH)
    keyval_matrix = w_keyval.reshape(D, H * 2 * DH)
    token_blocks = tokens.reshape(N_SEQ, TOK_DEV, D)
    offsets = jnp.arange(TOK_DEV, dtype=jnp.int32)
    ordered = offsets[:, None] >= offsets[None, :]

    def advance(carried_in, block_item):
        head_state, state_doc = carried_in
        token_block, block_index = block_item
        doc_ids = doc_index(block_index * TOK_DEV + offsets, doc_ends)
        queries = jax.nn.silu(jnp.dot(token_block, query_matrix, preferred_element_type=jnp.float32))
        queries = queries.astype(jnp.bfloat16).reshape(TOK_DEV, H, DH).astype(jnp.float32)
        keyval = jax.nn.silu(jnp.dot(token_block, keyval_matrix, preferred_element_type=jnp.float32))
        keyval = keyval.astype(jnp.bfloat16).reshape(TOK_DEV, H, 2 * DH).astype(jnp.float32)
        key_rows = keyval[:, :, :DH]
        values = keyval[:, :, DH:]
        same_doc = doc_ids[:, None] == doc_ids[None, :]
        causal = (ordered & same_doc).astype(jnp.float32)
        scores = jnp.einsum('thd,shd->hts', queries, key_rows, precision=high) * causal[None]
        weights = lax.optimization_barrier(scores.astype(jnp.bfloat16)).astype(jnp.float32)
        within = jnp.einsum('hts,she->the', weights, values, precision=high)
        state_rounded = lax.optimization_barrier(head_state.astype(jnp.bfloat16)).astype(jnp.float32)
        carried = jnp.einsum('thd,hde->the', queries, state_rounded, precision=high)
        carried = carried * (doc_ids == state_doc).astype(jnp.float32)[:, None, None]
        mixed = within + carried
        sum_squares = lax.optimization_barrier(jnp.sum(mixed * mixed, axis=(1, 2)))
        inverse_rms = lax.rsqrt(sum_squares / (H * DH) + 1e-06)
        output = (mixed.reshape(TOK_DEV, H * DH) * inverse_rms[:, None] * norm_gain.astype(jnp.float32)[None, :]).astype(jnp.bfloat16)
        tail_doc = doc_ids[TOK_DEV - 1]
        tail_mask = (doc_ids == tail_doc).astype(jnp.float32)
        tail_state = jnp.einsum('thd,the->hde', key_rows * tail_mask[:, None, None], values, precision=high)
        kept = (state_doc == tail_doc).astype(jnp.float32)
        return ((tail_state + kept * head_state, tail_doc), output)
    start = (jnp.zeros((H, DH, DH), jnp.float32), jnp.array(-1, dtype=jnp.int32))
    _, outputs = lax.scan(advance, start, (token_blocks, jnp.arange(N_SEQ, dtype=jnp.int32)))
    return outputs.reshape(TOKENS, H * DH)
```

```python
import functools

import jax
import jax.numpy as jnp
from jax import lax
from jax.experimental import pallas as pl
from jax.experimental.pallas import tpu as pltpu
from jax.sharding import PartitionSpec as P

MEMBERS = 4
VMEM = 60 * 1024 * 1024


def doc_index(positions, doc_ends):
    return jnp.sum((positions[:, None] >= doc_ends[None, :]).astype(jnp.int32), axis=1)


def silu(v):
    return v / (1.0 + jnp.exp(-v))


def params():
    return pltpu.CompilerParams(vmem_limit_bytes=VMEM)


def project_body(parts, steps, has_acc, has_buffer, activate, where_ref, k_ref, *refs):
    t_refs, refs = refs[:parts], refs[parts:]
    w_ref, refs = refs[0], refs[1:]
    if has_acc:
        start_ref, refs = refs[0], refs[1:]
    if has_buffer:
        refs = refs[1:]
    out_ref, total = refs
    step = pl.program_id(0)
    lhs = jnp.concatenate([r[...] for r in t_refs], axis=0) if parts > 1 else t_refs[0][...]
    product = jnp.dot(lhs, w_ref[...], preferred_element_type=jnp.float32)

    @pl.when(step == 0)
    def _():
        total[...] = product + start_ref[...] if has_acc else product

    @pl.when(step > 0)
    def _():
        total[...] += product

    @pl.when(step == steps - 1)
    def _():
        if not activate:
            out_ref[...] = total[...]
        else:
            rows = t_refs[0].shape[0]
            for e in range(parts):
                at = pl.multiple_of((where_ref[1] ^ e) * rows, 16) if parts > 1 else 0
                value = silu(total[pl.ds(e * rows, rows), :]).astype(out_ref.dtype)
                out_ref[0, pl.ds(at, rows), :] = value


def project(where, k_blocks, parts, w, depth, acc=None, buffer=None, place=0, activate=True):
    steps = k_blocks.shape[0]
    rows = sum(p.shape[0] for p in parts)
    width = w.shape[1]
    in_specs = [pl.BlockSpec((p.shape[0], depth), lambda k, wh, kb: (0, kb[k])) for p in parts]
    in_specs.append(pl.BlockSpec((depth, width), lambda k, wh, kb: (k, 0)))
    operands = list(parts) + [w]
    if acc is not None:
        in_specs.append(pl.BlockSpec((rows, width), lambda k, wh, kb: (0, 0)))
        operands.append(acc)
    aliases = {}
    if buffer is not None:
        aliases = {2 + len(operands): 0}
        in_specs.append(pl.BlockSpec(memory_space=pl.ANY))
        operands.append(buffer)
    if activate:
        out_shape = jax.ShapeDtypeStruct((MEMBERS, rows, width), jnp.bfloat16)
        out_spec = pl.BlockSpec((1, rows, width), lambda k, wh, kb: (wh[0] ^ place, 0, 0))
    else:
        out_shape = jax.ShapeDtypeStruct((rows, width), jnp.float32)
        out_spec = pl.BlockSpec((rows, width), lambda k, wh, kb: (0, 0))
    return pl.pallas_call(
        functools.partial(
            project_body, len(parts), steps, acc is not None, buffer is not None, activate
        ),
        grid_spec=pltpu.PrefetchScalarGridSpec(
            num_scalar_prefetch=2,
            grid=(steps,),
            in_specs=in_specs,
            out_specs=out_spec,
            scratch_shapes=[pltpu.VMEM((rows, width), jnp.float32)],
        ),
        out_shape=out_shape,
        input_output_aliases=aliases,
        compiler_params=params(),
        cost_estimate=pl.CostEstimate(
            flops=2 * rows * depth * steps * width,
            bytes_accessed=2 * depth * steps * (rows + width),
            transcendentals=0,
        ),
    )(where, k_blocks, *operands)


def doc_of(positions, ends_ref):
    total = jnp.zeros(positions.shape, jnp.int32)
    for i in range(ends_ref.shape[0]):
        total += (positions >= ends_ref[i]).astype(jnp.int32)
    return total


def doc_of_scalar(position, ends_ref):
    total = jnp.int32(0)
    for i in range(ends_ref.shape[0]):
        total += (position >= ends_ref[i]).astype(jnp.int32)
    return total


def tails_body(where_ref, ends_ref, kv_ref, tails_ref, state_ref):
    rows = kv_ref.shape[1]
    size = kv_ref.shape[2] // 2
    block = pl.program_id(1)
    start = (where_ref[2] * MEMBERS + block) * rows
    last = doc_of_scalar(start + rows - 1, ends_ref)
    before = doc_of_scalar(start - 1, ends_ref)
    docs = doc_of(start + lax.broadcasted_iota(jnp.int32, (rows, size), 0), ends_ref)
    keys = jnp.where(docs == last, kv_ref[0, :, :size].astype(jnp.float32), 0.0).astype(jnp.bfloat16)
    tail = lax.dot_general(
        keys, kv_ref[0, :, size:], (((0,), (0,)), ((), ())), preferred_element_type=jnp.float32
    )
    tails_ref[0, 0] = tail

    @pl.when(block == 0)
    def _():
        state_ref[0] = tail

    @pl.when(block > 0)
    def _():
        state_ref[0] = tail + jnp.where(before == last, 1.0, 0.0) * state_ref[0]


def tails(where, ends, kv, heads):
    blocks, rows, width = kv.shape
    size = width // heads // 2
    return pl.pallas_call(
        tails_body,
        grid_spec=pltpu.PrefetchScalarGridSpec(
            num_scalar_prefetch=2,
            grid=(heads, blocks),
            in_specs=[pl.BlockSpec((1, rows, 2 * size), lambda h, b, wh, en: (b, 0, h))],
            out_specs=[
                pl.BlockSpec((1, 1, size, size), lambda h, b, wh, en: (b, h, 0, 0)),
                pl.BlockSpec((1, size, size), lambda h, b, wh, en: (h, 0, 0)),
            ],
        ),
        out_shape=[
            jax.ShapeDtypeStruct((blocks, heads, size, size), jnp.float32),
            jax.ShapeDtypeStruct((heads, size, size), jnp.float32),
        ],
        compiler_params=params(),
        cost_estimate=pl.CostEstimate(
            flops=2 * blocks * rows * heads * size * size,
            bytes_accessed=2 * blocks * rows * width,
            transcendentals=0,
        ),
    )(where, ends, kv)


def attend_body(cut, where_ref, ends_ref, q_ref, kv_ref, tail_ref, entry_ref, out_ref, state):
    rows = kv_ref.shape[1]
    size = kv_ref.shape[2] // 2
    block = pl.program_id(1)
    start = (where_ref[2] * MEMBERS + block) * rows
    last = doc_of_scalar(start + rows - 1, ends_ref)
    before = doc_of_scalar(start - 1, ends_ref)

    @pl.when(block == 0)
    def _():
        state[...] = entry_ref[0]

    incoming = state[...].astype(jnp.bfloat16)
    row_docs = doc_of(start + lax.broadcasted_iota(jnp.int32, (1, rows), 1), ends_ref)
    for begin in range(0, rows, cut):
        seen = begin + cut
        q = q_ref[0, begin:seen, :]
        docs = doc_of(start + begin + lax.broadcasted_iota(jnp.int32, (cut, 1), 0), ends_ref)
        at = begin + lax.broadcasted_iota(jnp.int32, (cut, seen), 0)
        behind = lax.broadcasted_iota(jnp.int32, (cut, seen), 1)
        mask = (at >= behind) & (docs == row_docs[:, :seen])
        scores = lax.dot_general(
            q, kv_ref[0, :seen, :size], (((1,), (1,)), ((), ())), preferred_element_type=jnp.float32
        )
        weights = jnp.where(mask, scores, 0.0).astype(jnp.bfloat16)
        within = jnp.dot(weights, kv_ref[0, :seen, size:], preferred_element_type=jnp.float32)
        carried = jnp.dot(q, incoming, preferred_element_type=jnp.float32)
        out_ref[0, begin:seen, :] = within + jnp.where(docs == before, carried, 0.0)
    state[...] = tail_ref[0, 0] + jnp.where(before == last, 1.0, 0.0) * state[...]


def attend(where, ends, q, kv, tail, entry, heads):
    blocks, rows, width = q.shape
    size = width // heads
    cut = rows // 3 if rows % 48 == 0 else rows
    return pl.pallas_call(
        functools.partial(attend_body, cut),
        grid_spec=pltpu.PrefetchScalarGridSpec(
            num_scalar_prefetch=2,
            grid=(heads, blocks),
            in_specs=[
                pl.BlockSpec((1, rows, size), lambda h, b, wh, en: (b, 0, h)),
                pl.BlockSpec((1, rows, 2 * size), lambda h, b, wh, en: (b, 0, h)),
                pl.BlockSpec((1, 1, size, size), lambda h, b, wh, en: (b, h, 0, 0)),
                pl.BlockSpec((1, size, size), lambda h, b, wh, en: (h, 0, 0)),
            ],
            out_specs=pl.BlockSpec((1, rows, size), lambda h, b, wh, en: (b, 0, h)),
            scratch_shapes=[pltpu.VMEM((size, size), jnp.float32)],
        ),
        out_shape=jax.ShapeDtypeStruct((blocks, rows, width), jnp.float32),
        compiler_params=params(),
        cost_estimate=pl.CostEstimate(
            flops=3 * blocks * rows * rows * heads * size,
            bytes_accessed=12 * blocks * rows * width,
            transcendentals=0,
        ),
    )(where, ends, q, kv, tail, entry)


def place_body(where_ref, *refs):
    out_ref = refs[-1]
    for k in range(MEMBERS):

        @pl.when(pl.program_id(0) == k)
        def _():
            out_ref[...] = refs[k][...]


def place(where, parts):
    rows, width = parts[0].shape
    return pl.pallas_call(
        place_body,
        grid_spec=pltpu.PrefetchScalarGridSpec(
            num_scalar_prefetch=1,
            grid=(MEMBERS,),
            in_specs=[pl.BlockSpec((rows, width), lambda k, wh: (0, 0)) for _ in parts],
            out_specs=pl.BlockSpec((rows, width), lambda k, wh: (0, wh[0] ^ k)),
        ),
        out_shape=jax.ShapeDtypeStruct((rows, MEMBERS * width), parts[0].dtype),
        compiler_params=params(),
    )(where, *parts)


def after(value, *others):
    return lax.optimization_barrier((value, *others))[0]


def grouped(seq_size, fsdp_size, tokens, w_query, w_keyval, doc_lengths, norm_gain):
    rows, model = tokens.shape
    depth, head_count, size = w_query.shape
    heads = head_count // MEMBERS
    groups = seq_size // MEMBERS
    s = lax.axis_index("seq")
    f = lax.axis_index("fsdp")
    m = lax.rem(s, MEMBERS)
    g = lax.div(s, MEMBERS)
    where = jnp.stack([m, f, g]).astype(jnp.int32)
    doc_ends = jnp.cumsum(doc_lengths)

    def hop(value, k):
        return lax.ppermute(value, "seq", [(i, i ^ k) for i in range(seq_size)])

    def side(value, k):
        return lax.ppermute(value, "fsdp", [(i, i ^ k) for i in range(fsdp_size)])

    q_width, kv_width = heads * size, 2 * heads * size
    wq = w_query.reshape(depth, head_count * size)
    wkv = w_keyval.reshape(depth, head_count * 2 * size)

    def columns(k):
        at = m ^ k
        return (
            lax.dynamic_slice(wkv, (0, at * kv_width), (depth, kv_width)),
            lax.dynamic_slice(wq, (0, at * q_width), (depth, q_width)),
        )

    kv_a, q_a = columns(0)
    kv_b, q_b = columns(2)
    kv_c, q_c = columns(1)
    kv_d, q_d = columns(3)
    piece_rows = rows // fsdp_size
    own_piece = lax.dynamic_slice(tokens, (f * piece_rows, 0), (piece_rows, model))

    kv = {0: kv_a}
    q = {0: q_a}

    first = 4
    kv[4] = hop(kv_a, 4)
    q[6] = hop(q_b, 6)
    tz = hop(own_piece, 2)
    tx = hop(own_piece, 1)

    kv[1] = hop(after(kv_c, tx), 1)
    kvx_b = hop(after(kv_d, tx), 1)
    q[1] = hop(after(q_c, kv[1]), 1)
    qx_b = hop(after(q_d, kvx_b), 1)
    tzx = hop(after(tz, q[1], qx_b), 1)

    kv[6] = hop(after(kv_b, q[6]), 6)
    q[4] = hop(after(q_a, kv[4]), 4)
    kv[5] = hop(after(kv[1], q[4]), 4)
    kv[7] = hop(after(kvx_b, kv[6]), 6)
    q[5] = hop(after(q[1], kv[5]), 4)
    q[7] = hop(after(qx_b, kv[7]), 6)

    kv[2] = hop(after(kv_b, tz), 2)
    kv[3] = hop(after(kvx_b, kv[2]), 2)
    q[2] = hop(after(q_b, kv[3]), 2)
    q[3] = hop(after(qx_b, q[2]), 2)

    def spread(piece, *waits):
        pieces = [after(piece, *waits)] if waits else [piece]
        bit = fsdp_size // 2
        found = {0: pieces[0]}
        while bit >= 1:
            for e in sorted(found):
                found[e | bit] = side(found[e], bit)
            bit //= 2
        return [found[e] for e in range(fsdp_size)]

    px = spread(tx)
    pz = spread(tz, px[2])
    pzx = spread(tzx, pz[2])
    parts = {0: [tokens], 1: px, 2: pz, 3: pzx}

    total = sorted(kv)
    w_kv = jnp.concatenate([kv[k] for k in total], axis=0)
    k_all = jnp.stack([s ^ k for k in total]).astype(jnp.int32)
    early = [k for k in total if k not in (5, 7)]
    late = [5, 7]
    w_q_early = jnp.concatenate([q[k] for k in early], axis=0)
    w_q_late = jnp.concatenate([q[k] for k in late], axis=0)
    k_early = jnp.stack([s ^ k for k in early]).astype(jnp.int32)
    k_late = jnp.stack([s ^ k for k in late]).astype(jnp.int32)

    keyval = None
    for j in range(MEMBERS):
        keyval = project(where, k_all, parts[j], w_kv, depth, buffer=keyval, place=j)
    tail, state = tails(where, doc_ends, keyval, heads)
    entry = jnp.zeros_like(state)
    edge_doc = doc_index(g[None] * MEMBERS * rows - 1, doc_ends)[0]
    for k in range(1, groups):
        other = hop(state, MEMBERS * k)
        owner = g ^ k
        owner_doc = doc_index((owner[None] + 1) * MEMBERS * rows - 1, doc_ends)[0]
        entry += jnp.where((owner < g) & (owner_doc == edge_doc), other, 0.0)

    queries = None
    for j in range(MEMBERS):
        acc = project(where, k_early, parts[j], w_q_early, depth, activate=False)
        queries = project(
            where, k_late, parts[j], w_q_late, depth, acc=acc, buffer=queries, place=j
        )
    mixed = attend(where, doc_ends, queries, keyval, tail, entry, heads)

    sums = lax.psum(jnp.sum(mixed * mixed, axis=2), "fsdp")
    sums = sums + hop(sums, 1)
    sums = sums + hop(sums, 2)
    inverse = lax.rsqrt(sums / (head_count * fsdp_size * size) + 1e-06)
    gain = lax.dynamic_slice(norm_gain, (m * q_width,), (q_width,)).astype(jnp.float32)
    normed = (mixed * inverse[:, :, None] * gain[None, None, :]).astype(jnp.bfloat16)
    outs = []
    for k in range(MEMBERS):
        part = lax.dynamic_index_in_dim(normed, m ^ k, 0, keepdims=False)
        outs.append(hop(part, k) if k else part)
    return place(where, outs)


def plain(tokens, w_query, w_keyval, doc_lengths, norm_gain):
    rows_here = tokens.shape[0]
    head_count = w_query.shape[1]
    head_size = w_query.shape[2]
    shard_index = lax.axis_index("seq")
    doc_ends = jnp.cumsum(doc_lengths)
    offsets = lax.iota(jnp.int32, rows_here)
    doc_ids = doc_index(shard_index * rows_here + offsets, doc_ends)
    first_doc = doc_ids[0]
    tail_doc = doc_ids[rows_here - 1]

    def project(panel_rows):
        panel = panel_rows.reshape(panel_rows.shape[0], panel_rows.shape[1] * panel_rows.shape[2])
        return jnp.dot(tokens, panel, preferred_element_type=jnp.float32)

    query_sum = project(lax.all_gather(w_query, "seq", axis=0, tiled=True))
    keyval_sum = project(lax.all_gather(w_keyval, "seq", axis=0, tiled=True))
    keyval = (
        jax.nn.silu(keyval_sum).astype(jnp.bfloat16).reshape(rows_here, head_count, 2 * head_size)
    )
    key_rows = keyval[:, :, :head_size]
    values = keyval[:, :, head_size:]
    tail_mask = (doc_ids == tail_doc).astype(jnp.bfloat16)
    tail_state = jnp.einsum(
        "thd,the->hde",
        key_rows * tail_mask[:, None, None],
        values,
        preferred_element_type=jnp.float32,
    )
    states = lax.all_gather(tail_state[None], "seq", axis=0, tiled=True)
    shard_ids = lax.iota(jnp.int32, states.shape[0])
    owner_docs = doc_index(shard_ids * rows_here + rows_here - 1, doc_ends)
    selected = ((shard_ids < shard_index) & (owner_docs == first_doc)).astype(jnp.float32)
    incoming = jnp.sum(selected[:, None, None, None] * states, axis=0)
    queries = jax.nn.silu(query_sum).astype(jnp.bfloat16).reshape(rows_here, head_count, head_size)
    scores = jnp.einsum("thd,shd->hts", queries, key_rows, preferred_element_type=jnp.float32)
    causal = (
        (offsets[:, None] >= offsets[None, :]) & (doc_ids[:, None] == doc_ids[None, :])
    ).astype(jnp.float32)
    weights = (scores * causal[None]).astype(jnp.bfloat16)
    within = jnp.einsum("hts,she->the", weights, values, preferred_element_type=jnp.float32)
    carried = jnp.einsum(
        "thd,hde->the", queries, incoming.astype(jnp.bfloat16), preferred_element_type=jnp.float32
    )
    carried = carried * (doc_ids == first_doc).astype(jnp.float32)[:, None, None]
    mixed = within + carried
    sum_squares = lax.psum(jnp.sum(mixed * mixed, axis=(1, 2)), "fsdp")
    inverse_rms = lax.rsqrt(sum_squares / (head_count * lax.axis_size("fsdp") * head_size) + 1e-06)
    flat = mixed.reshape(rows_here, head_count * head_size)
    return (flat * inverse_rms[:, None] * norm_gain.astype(jnp.float32)[None, :]).astype(
        jnp.bfloat16
    )


def solution(mesh):
    seq_size, fsdp_size = mesh.shape["seq"], mesh.shape["fsdp"]
    if seq_size == 2 * MEMBERS:
        body = functools.partial(grouped, seq_size, fsdp_size)
    else:
        body = plain
    return jax.shard_map(
        body,
        mesh=mesh,
        in_specs=(P("seq", None), P("seq", "fsdp", None), P("seq", "fsdp", None), P(), P("fsdp")),
        out_specs=P("seq", "fsdp"),
        check_vma=False,
    )
```

```python
import functools

import jax
import jax.numpy as jnp
from jax import lax
from jax.experimental import pallas as pl
from jax.experimental.pallas import tpu as pltpu
from jax.sharding import PartitionSpec as P

MEMBERS = 4
VMEM = 60 * 1024 * 1024


def doc_index(positions, doc_ends):
    return jnp.sum((positions[:, None] >= doc_ends[None, :]).astype(jnp.int32), axis=1)


def silu(v):
    return v / (1.0 + jnp.exp(-v))


def params():
    return pltpu.CompilerParams(vmem_limit_bytes=VMEM)


def project_body(places, fsdp_size, steps, starts, activate, where_ref, k_ref, *refs):
    parts = len(places)
    t_refs, w_ref, start_refs, out_ref = refs[:parts], refs[parts], refs[parts + 1 : -1], refs[-1]
    total = out_ref
    if activate:
        start_refs, out_ref, total = refs[parts + 1 : -2], refs[-2], refs[-1]
    step = pl.program_id(0)
    lhs = jnp.concatenate([r[...] for r in t_refs], axis=0) if parts > 1 else t_refs[0][...]
    product = jnp.dot(lhs, w_ref[...], preferred_element_type=jnp.float32)

    @pl.when(step == 0)
    def _():
        if not starts:
            total[...] = product
        at = 0
        for ref in start_refs:
            rows = ref.shape[0]
            total[at : at + rows, :] = product[at : at + rows] + ref[...]
            at += rows

    @pl.when(step > 0)
    def _():
        total[...] += product

    if activate:

        @pl.when(step == steps - 1)
        def _():
            m, f = where_ref[0], where_ref[1]
            block_rows = out_ref.shape[0] // MEMBERS
            at = 0
            for ref, (j, spots) in zip(t_refs, places):
                rows = ref.shape[0] // len(spots)
                for e, offset in spots:
                    to = (m ^ j) * block_rows
                    if e is not None:
                        to = to + (f ^ e) * (block_rows // fsdp_size) + offset
                    to = pl.multiple_of(to, 16)
                    value = silu(total[at : at + rows, :])
                    out_ref[pl.ds(to, rows), :] = value.astype(out_ref.dtype)
                    at += rows


def part_rows(part, depth):
    return part.shape[0] * part.shape[1] // (depth * lax.axis_size("seq"))


def part_spec(part, depth, block):
    if part.shape[1] == depth:
        return pl.BlockSpec((part_rows(part, depth), depth), lambda *a: (block(*a), 0))
    return pl.BlockSpec((part.shape[0], depth), lambda *a: (0, block(*a)))


def project(where, k_blocks, parts, w, column, width, starts=(), start_column=0, activate=True):
    steps = k_blocks.shape[0]
    depth = w.shape[0] // steps
    rows = sum(part_rows(p, depth) for p, _ in parts)
    in_specs = [part_spec(p, depth, lambda k, wh, kb: kb[k]) for p, _ in parts]
    in_specs.append(pl.BlockSpec((depth, width), lambda k, wh, kb: (k, column)))
    in_specs += [
        pl.BlockSpec((a.shape[0], width), lambda k, wh, kb: (0, start_column)) for a in starts
    ]
    kind = jnp.bfloat16 if activate else jnp.float32
    return pl.pallas_call(
        functools.partial(
            project_body, [p for _, p in parts], lax.axis_size("fsdp"), steps, len(starts), activate
        ),
        grid_spec=pltpu.PrefetchScalarGridSpec(
            num_scalar_prefetch=2,
            grid=(steps,),
            in_specs=in_specs,
            out_specs=pl.BlockSpec((rows, width), lambda k, wh, kb: (0, 0)),
            scratch_shapes=[pltpu.VMEM((rows, width), jnp.float32)] if activate else [],
        ),
        out_shape=jax.ShapeDtypeStruct((rows, width), kind),
        compiler_params=params(),
        cost_estimate=pl.CostEstimate(
            flops=2 * rows * depth * steps * width,
            bytes_accessed=2 * depth * steps * (rows + width),
            transcendentals=0,
        ),
    )(where, k_blocks, *[p for p, _ in parts], w, *starts)


def doc_of(positions, ends_ref):
    total = jnp.zeros(positions.shape, jnp.int32)
    for i in range(ends_ref.shape[0]):
        total += (positions >= ends_ref[i]).astype(jnp.int32)
    return total


def doc_of_scalar(position, ends_ref):
    total = jnp.int32(0)
    for i in range(ends_ref.shape[0]):
        total += (position >= ends_ref[i]).astype(jnp.int32)
    return total


def tails_body(heads, where_ref, ends_ref, kv_ref, tails_ref, state_ref):
    rows = kv_ref.shape[1]
    size = kv_ref.shape[2] // heads // 2
    block = pl.program_id(0)
    start = (where_ref[2] * MEMBERS + block) * rows
    last = doc_of_scalar(start + rows - 1, ends_ref)
    before = doc_of_scalar(start - 1, ends_ref)
    docs = doc_of(start + lax.broadcasted_iota(jnp.int32, (rows, size), 0), ends_ref)
    kept = jnp.where((before == last) & (block > 0), 1.0, 0.0)
    for h in range(heads):
        at = 2 * h * size
        keys = kv_ref[0, :, at : at + size].astype(jnp.float32)
        keys = jnp.where(docs == last, keys, 0.0).astype(jnp.bfloat16)
        values = kv_ref[0, :, at + size : at + 2 * size]
        tail = lax.dot_general(
            keys, values, (((0,), (0,)), ((), ())), preferred_element_type=jnp.float32
        )
        tails_ref[0, h] = tail

        @pl.when(block == 0)
        def _():
            state_ref[h] = tail

        @pl.when(block > 0)
        def _():
            state_ref[h] = tail + kept * state_ref[h]


def tails(where, ends, kv, heads):
    blocks, rows, width = kv.shape
    size = width // heads // 2
    return pl.pallas_call(
        functools.partial(tails_body, heads),
        grid_spec=pltpu.PrefetchScalarGridSpec(
            num_scalar_prefetch=2,
            grid=(blocks,),
            in_specs=[pl.BlockSpec((1, rows, width), lambda b, wh, en: (b, 0, 0))],
            out_specs=[
                pl.BlockSpec((1, heads, size, size), lambda b, wh, en: (b, 0, 0, 0)),
                pl.BlockSpec((heads, size, size), lambda b, wh, en: (0, 0, 0)),
            ],
        ),
        out_shape=[
            jax.ShapeDtypeStruct((blocks, heads, size, size), jnp.float32),
            jax.ShapeDtypeStruct((heads, size, size), jnp.float32),
        ],
        compiler_params=params(),
        cost_estimate=pl.CostEstimate(
            flops=2 * blocks * rows * heads * size * size,
            bytes_accessed=2 * blocks * rows * width,
            transcendentals=0,
        ),
    )(where, ends, kv)


def incoming_body(rows, where_ref, ends_ref, tails_ref, other_ref, out_ref):
    blocks = tails_ref.shape[0]
    g = where_ref[2]
    start = g * blocks * rows
    edge = doc_of_scalar(start - 1, ends_ref)
    owner = doc_of_scalar((g ^ 1) * blocks * rows + blocks * rows - 1, ends_ref)
    state = jnp.where((g == 1) & (owner == edge), 1.0, 0.0) * other_ref[...]
    for b in range(blocks):
        out_ref[b] = state.astype(out_ref.dtype)
        before = doc_of_scalar(start + b * rows - 1, ends_ref)
        last = doc_of_scalar(start + (b + 1) * rows - 1, ends_ref)
        state = tails_ref[b] + jnp.where(before == last, 1.0, 0.0) * state


def incoming_states(where, ends, tail, other, rows):
    return pl.pallas_call(
        functools.partial(incoming_body, rows),
        grid_spec=pltpu.PrefetchScalarGridSpec(
            num_scalar_prefetch=2,
            grid=(1,),
            in_specs=[
                pl.BlockSpec(tail.shape, lambda i, wh, en: (0, 0, 0, 0)),
                pl.BlockSpec(other.shape, lambda i, wh, en: (0, 0, 0)),
            ],
            out_specs=pl.BlockSpec(tail.shape, lambda i, wh, en: (0, 0, 0, 0)),
        ),
        out_shape=jax.ShapeDtypeStruct(tail.shape, jnp.bfloat16),
        compiler_params=params(),
    )(where, ends, tail, other)


def attend_body(
    places, fsdp_size, steps, heads, cut, where_ref, ends_ref, k_ref, *refs
):
    parts = len(places)
    t_refs = refs[:parts]
    w_ref, start_ref, kv_ref, state_ref, out_ref, square_ref, total, q_ref = refs[parts:]
    step = pl.program_id(0)
    lhs = jnp.concatenate([r[...] for r in t_refs], axis=0) if parts > 1 else t_refs[0][...]
    product = jnp.dot(lhs, w_ref[...], preferred_element_type=jnp.float32)

    @pl.when(step == 0)
    def _():
        total[...] = product + start_ref[...]

    @pl.when(step > 0)
    def _():
        total[...] += product

    @pl.when(step == steps - 1)
    def _():
        m, f, g = where_ref[0], where_ref[1], where_ref[2]
        rows, width = q_ref.shape
        size = width // heads
        place = places[0][0]
        at = 0
        for ref, (_, spots) in zip(t_refs, places):
            count = ref.shape[0] // len(spots)
            for e, offset in spots:
                to = 0
                if e is not None:
                    to = pl.multiple_of((f ^ e) * (rows // fsdp_size) + offset, 16)
                q_ref[pl.ds(to, count), :] = silu(total[at : at + count, :]).astype(q_ref.dtype)
                at += count
        start = (g * MEMBERS + (m ^ place)) * rows
        before = doc_of_scalar(start - 1, ends_ref)
        row_docs = doc_of(start + lax.broadcasted_iota(jnp.int32, (1, rows), 1), ends_ref)
        for begin in range(0, rows, cut):
            seen = begin + cut
            docs = doc_of(start + begin + lax.broadcasted_iota(jnp.int32, (cut, 1), 0), ends_ref)
            at = begin + lax.broadcasted_iota(jnp.int32, (cut, seen), 0)
            behind = lax.broadcasted_iota(jnp.int32, (cut, seen), 1)
            mask = (at >= behind) & (docs == row_docs[:, :seen])
            mixed = []
            for h in range(heads):
                k_at, v_at = 2 * h * size, (2 * h + 1) * size
                q = q_ref[begin:seen, h * size : (h + 1) * size]
                scores = lax.dot_general(
                    q, kv_ref[0, :seen, k_at : k_at + size], (((1,), (1,)), ((), ())),
                    preferred_element_type=jnp.float32,
                )
                weights = jnp.where(mask, scores, 0.0).astype(jnp.bfloat16)
                within = jnp.dot(
                    weights, kv_ref[0, :seen, v_at : v_at + size],
                    preferred_element_type=jnp.float32,
                )
                carried = jnp.dot(q, state_ref[0, h], preferred_element_type=jnp.float32)
                mixed.append(within + jnp.where(docs == before, carried, 0.0))
            mixed = jnp.concatenate(mixed, axis=1)
            out_ref[begin:seen, :] = mixed.astype(out_ref.dtype)
            square_ref[:, begin:seen] = lax.dot_general(
                jnp.ones((8, width), jnp.float32), mixed * mixed, (((1,), (1,)), ((), ())),
                precision=lax.Precision.HIGHEST, preferred_element_type=jnp.float32,
            )


def attend(where, ends, k_blocks, parts, w, acc, acc_at, acc_column, kv, states):
    steps = k_blocks.shape[0]
    depth, width = w.shape[0] // steps, w.shape[1]
    heads = states.shape[1]
    rows = kv.shape[1]
    size = width // heads
    place = parts[0][1][0]
    cut = rows // 3 if rows % 384 == 0 else rows
    in_specs = [part_spec(p, depth, lambda k, wh, en, kb: kb[k]) for p, _ in parts]
    in_specs += [
        pl.BlockSpec((depth, width), lambda k, wh, en, kb: (k, 0)),
        pl.BlockSpec((rows, width), lambda k, wh, en, kb: (acc_at, acc_column)),
        pl.BlockSpec((1, rows, kv.shape[2]), lambda k, wh, en, kb: (wh[0] ^ place, 0, 0)),
        pl.BlockSpec((1, heads, size, size), lambda k, wh, en, kb: (wh[0] ^ place, 0, 0, 0)),
    ]
    return pl.pallas_call(
        functools.partial(
            attend_body, [p for _, p in parts], lax.axis_size("fsdp"), steps, heads, cut
        ),
        grid_spec=pltpu.PrefetchScalarGridSpec(
            num_scalar_prefetch=3,
            grid=(steps,),
            in_specs=in_specs,
            out_specs=[
                pl.BlockSpec((rows, width), lambda k, wh, en, kb: (0, 0)),
                pl.BlockSpec((8, rows), lambda k, wh, en, kb: (0, 0)),
            ],
            scratch_shapes=[
                pltpu.VMEM((rows, width), jnp.float32),
                pltpu.VMEM((rows, width), jnp.bfloat16),
            ],
        ),
        out_shape=[
            jax.ShapeDtypeStruct((rows, width), jnp.bfloat16),
            jax.ShapeDtypeStruct((8, rows), jnp.float32),
        ],
        compiler_params=params(),
        cost_estimate=pl.CostEstimate(
            flops=2 * rows * depth * steps * width + 3 * rows * rows * width,
            bytes_accessed=2 * depth * steps * (rows + width) + 12 * rows * width,
            transcendentals=rows * width,
        ),
    )(where, ends, k_blocks, *[p for p, _ in parts], w, acc, kv, states)


def finish_body(where_ref, *refs):
    inverse_ref, gain_ref, out_ref = refs[MEMBERS:]
    width = refs[0].shape[1]
    for k in range(MEMBERS):
        at = pl.multiple_of((where_ref[0] ^ k) * width, width)
        gain = gain_ref[:, pl.ds(at, width)].astype(jnp.float32)
        value = refs[k][...].astype(jnp.float32) * inverse_ref[...] * gain
        out_ref[:, pl.ds(at, width)] = value.astype(out_ref.dtype)


def finish(where, parts, inverse, gain):
    rows, width = parts[0].shape
    whole = lambda shape: pl.BlockSpec(shape, lambda i, wh: (0, 0))
    return pl.pallas_call(
        finish_body,
        grid_spec=pltpu.PrefetchScalarGridSpec(
            num_scalar_prefetch=1,
            grid=(1,),
            in_specs=[whole((rows, width)) for _ in parts]
            + [whole((rows, 1)), whole((1, MEMBERS * width))],
            out_specs=whole((rows, MEMBERS * width)),
        ),
        out_shape=jax.ShapeDtypeStruct((rows, MEMBERS * width), jnp.bfloat16),
        compiler_params=params(),
    )(where, *parts, inverse, gain)


def grouped(seq_size, fsdp_size, tokens, w_query, w_keyval, doc_lengths, norm_gain):
    rows, model = tokens.shape
    depth, head_count, size = w_query.shape
    heads = head_count // MEMBERS
    s = lax.axis_index("seq")
    f = lax.axis_index("fsdp")
    m = lax.rem(s, MEMBERS)
    g = lax.div(s, MEMBERS)
    where = jnp.stack([m, f, g]).astype(jnp.int32)
    doc_ends = jnp.cumsum(doc_lengths)

    inner = ((s >> 1) ^ (s >> 2)) & 1 == 1
    inner_seq = [i for i in range(seq_size) if ((i >> 1) ^ (i >> 2)) & 1 == 1]
    outer_seq = [i for i in range(seq_size) if i not in inner_seq]

    def hop(value, k, only=range(seq_size)):
        return lax.ppermute(value, "seq", [(i, i ^ k) for i in only])

    def side(value, k):
        return lax.ppermute(value, "fsdp", [(i, i ^ k) for i in range(fsdp_size)])

    q_width, kv_width = heads * size, 2 * heads * size
    width = kv_width + q_width
    q_block = kv_width // q_width
    flat_kv = w_keyval.reshape(depth, head_count * 2 * size)
    flat_q = w_query.reshape(depth, head_count * size)

    def columns(k):
        at = m ^ k
        return jnp.concatenate(
            [
                lax.dynamic_slice(flat_kv, (0, at * kv_width), (depth, kv_width)),
                lax.dynamic_slice(flat_q, (0, at * q_width), (depth, q_width)),
            ],
            axis=1,
        )

    half = rows // fsdp_size // 2

    def own(i):
        chunk = lax.dynamic_slice(tokens, ((2 * f + i) * half, 0), (half, model))
        return chunk.reshape(half, seq_size, depth).transpose(1, 0, 2).reshape(-1, depth)

    def stage(done, operands):
        return lax.optimization_barrier((tuple(operands), tuple(done)))[0]

    def blocks(ks):
        return jnp.stack([s ^ k for k in ks]).astype(jnp.int32)

    def pairs(inner_hop, outer_hop):
        moves = [(i, i ^ inner_hop) for i in inner_seq if inner_hop]
        moves += [(i, i ^ outer_hop) for i in outer_seq if outer_hop]
        return lambda value: lax.ppermute(value, "seq", moves)

    def pick(a, b):
        return jnp.where(inner, a, b)

    def spread(j, first, second):
        found = []
        for offset, pieces in ((0, first), (half, second)):
            found += [(p, (j, [(e, offset)])) for e, p in zip((0, 2, 1, 3), pieces)]
        return found

    def x(value):
        return hop(value, 1)

    def y(value):
        return side(value, 2)

    def c(value):
        return side(value, 1)

    both_ways = pairs(2, 2)
    own1 = own(0)
    tz1 = both_ways(own1)
    tx1 = x(own1)
    wb = columns(2)
    r1 = pairs(6, 0)(wb)
    wa, wc, wd, own2 = columns(0), columns(1), columns(3), own(1)
    in2, in3 = pick(wa, own2), pick(own2, wa)
    o = stage([r1, tz1, tx1, wc, wd, own2, in3], [in2, own2, tx1, tx1, tz1])
    r2 = pairs(4, 2)(o[0])
    tx2 = x(o[1])
    yx1 = y(o[2])
    cx1 = c(o[3])
    cz1 = c(o[4])
    o = stage([r2, tx2, yx1, cx1, cz1], [in3, wd, tx2, tx2, yx1])
    r3 = pairs(2, 4)(o[0])
    rxb = x(o[1])
    yx2 = y(o[2])
    cx2 = c(o[3])
    dx1 = c(o[4])
    o = stage([r3, rxb, yx2, cx2, dx1], [wb, tz1, tz1, yx2])
    r4 = pairs(0, 6)(o[0])
    tzx1 = x(o[1])
    yz1 = y(o[2])
    dx2 = c(o[3])
    tz2 = pick(r2, r3)
    w4 = pick(r3, r2)
    o = stage([r4, tzx1, yz1, dx2, tz2, w4], [rxb, wb, wc, tzx1, yz1])
    r5 = pairs(6, 0)(o[0])
    z5 = both_ways(o[1])
    rxa = x(o[2])
    yzx1 = y(o[3])
    dz1 = c(o[4])
    w6 = pick(r1, r4)
    o = stage([r5, z5, rxa, yzx1, dz1, w6], [pick(rxa, rxb), tz2, tz2, tzx1, yzx1])
    r6 = pairs(4, 2)(o[0])
    tzx2 = x(o[1])
    yz2 = y(o[2])
    czx1 = c(o[3])
    dzx1 = c(o[4])
    in7 = pick(rxb, rxa)
    in7_kv, in7_q = in7[:, :kv_width], in7[:, kv_width:]
    rxb_kv, rxb_q = rxb[:, :kv_width], rxb[:, kv_width:]
    w_early = jnp.concatenate([wa, rxa, z5, w4, w6], axis=0)
    early = [0, 1, 2, 4, 6]
    part0 = [(tokens, (0, [(None, 0)]))]
    part1 = spread(1, (tx1, yx1, cx1, dx1), (tx2, yx2, cx2, dx2))
    acc01 = project(where, blocks(early), part0 + part1, w_early, 0, width, activate=False)
    o = stage(
        [r6, tzx2, yz2, czx1, dzx1, acc01, rxb_kv, rxb_q, in7_q], [in7_kv, tzx2, tz2, tzx2, yz2]
    )
    r7 = pairs(2, 4)(o[0])
    yzx2 = y(o[1])
    cz2 = c(o[2])
    czx2 = c(o[3])
    dz2 = c(o[4])
    sixth = s ^ pick(3, 5)
    acc01 = project(
        where, sixth[None].astype(jnp.int32), part0 + part1, r6, 0, width,
        starts=(acc01,), activate=False,
    )
    w_more = jnp.concatenate([w_early, r6], axis=0)
    k_more = jnp.concatenate([blocks(early), sixth[None].astype(jnp.int32)])
    o = stage([r7, yzx2, cz2, czx2, dz2, acc01, w_more], [rxb_kv, yzx2])
    r8 = pairs(0, 6)(o[0])
    dzx2 = c(o[1])
    part2 = spread(2, (tz1, yz1, cz1, dz1), (tz2, yz2, cz2, dz2))
    acc2 = project(where, k_more, part2, w_more, 0, width, activate=False)
    o = stage([r8, dzx2, acc2], [in7_q, rxb_q])
    r7q = pairs(2, 4)(o[0])
    r8q = pairs(0, 6)(o[1])
    part3 = spread(3, (tzx1, yzx1, czx1, dzx1), (tzx2, yzx2, czx2, dzx2))
    acc3 = project(where, k_more, part3, w_more, 0, width, activate=False)

    accs = (acc01, acc2, acc3)
    all_parts = part0 + part1 + part2 + part3
    last = jnp.stack([s ^ pick(5, 3), s ^ 7]).astype(jnp.int32)
    w_late = jnp.concatenate([r7, pick(r5[:, :kv_width], r8)], axis=0)
    keyval = project(where, last, all_parts, w_late, 0, kv_width, starts=accs)
    keyval = keyval.reshape(MEMBERS, rows, kv_width)
    tail, state = tails(where, doc_ends, keyval, heads)
    other = hop(state, MEMBERS)
    states = incoming_states(where, doc_ends, tail, other, rows)

    w_last = jnp.concatenate([r7q, pick(r5[:, kv_width:], r8q)], axis=0)
    outs, squares = {}, 0.0
    before = ()
    for k, part, acc, acc_at in (
        (3, part3, acc3, 0), (2, part2, acc2, 0), (1, part1, acc01, 1), (0, part0, acc01, 0)
    ):
        if before:
            w_last = stage(before, [w_last])[0]
        outs[k], square = attend(
            where, doc_ends, last, part, w_last, acc, acc_at, q_block, keyval, states
        )
        before = (outs[k],)
        if k:
            outs[k], square = hop(outs[k], k), hop(square[:1], k)
        else:
            square = square[:1]
        squares = squares + square
    squares = squares + side(squares, 2)
    squares = squares + side(squares, 1)
    inverse = lax.rsqrt(squares / (head_count * fsdp_size * size) + 1e-06).reshape(rows, 1)
    return finish(where, [outs[k] for k in range(MEMBERS)], inverse, norm_gain[None, :])


def plain(tokens, w_query, w_keyval, doc_lengths, norm_gain):
    rows_here = tokens.shape[0]
    head_count = w_query.shape[1]
    head_size = w_query.shape[2]
    shard_index = lax.axis_index("seq")
    doc_ends = jnp.cumsum(doc_lengths)
    offsets = lax.iota(jnp.int32, rows_here)
    doc_ids = doc_index(shard_index * rows_here + offsets, doc_ends)
    first_doc = doc_ids[0]
    tail_doc = doc_ids[rows_here - 1]

    def project(panel_rows):
        panel = panel_rows.reshape(panel_rows.shape[0], panel_rows.shape[1] * panel_rows.shape[2])
        return jnp.dot(tokens, panel, preferred_element_type=jnp.float32)

    query_sum = project(lax.all_gather(w_query, "seq", axis=0, tiled=True))
    keyval_sum = project(lax.all_gather(w_keyval, "seq", axis=0, tiled=True))
    keyval = (
        jax.nn.silu(keyval_sum).astype(jnp.bfloat16).reshape(rows_here, head_count, 2 * head_size)
    )
    key_rows = keyval[:, :, :head_size]
    values = keyval[:, :, head_size:]
    tail_mask = (doc_ids == tail_doc).astype(jnp.bfloat16)
    tail_state = jnp.einsum(
        "thd,the->hde",
        key_rows * tail_mask[:, None, None],
        values,
        preferred_element_type=jnp.float32,
    )
    states = lax.all_gather(tail_state[None], "seq", axis=0, tiled=True)
    shard_ids = lax.iota(jnp.int32, states.shape[0])
    owner_docs = doc_index(shard_ids * rows_here + rows_here - 1, doc_ends)
    selected = ((shard_ids < shard_index) & (owner_docs == first_doc)).astype(jnp.float32)
    incoming = jnp.sum(selected[:, None, None, None] * states, axis=0)
    queries = jax.nn.silu(query_sum).astype(jnp.bfloat16).reshape(rows_here, head_count, head_size)
    scores = jnp.einsum("thd,shd->hts", queries, key_rows, preferred_element_type=jnp.float32)
    causal = (
        (offsets[:, None] >= offsets[None, :]) & (doc_ids[:, None] == doc_ids[None, :])
    ).astype(jnp.float32)
    weights = (scores * causal[None]).astype(jnp.bfloat16)
    within = jnp.einsum("hts,she->the", weights, values, preferred_element_type=jnp.float32)
    carried = jnp.einsum(
        "thd,hde->the", queries, incoming.astype(jnp.bfloat16), preferred_element_type=jnp.float32
    )
    carried = carried * (doc_ids == first_doc).astype(jnp.float32)[:, None, None]
    mixed = within + carried
    sum_squares = lax.psum(jnp.sum(mixed * mixed, axis=(1, 2)), "fsdp")
    inverse_rms = lax.rsqrt(sum_squares / (head_count * lax.axis_size("fsdp") * head_size) + 1e-06)
    flat = mixed.reshape(rows_here, head_count * head_size)
    return (flat * inverse_rms[:, None] * norm_gain.astype(jnp.float32)[None, :]).astype(
        jnp.bfloat16
    )


def solution(mesh):
    seq_size, fsdp_size = mesh.shape["seq"], mesh.shape["fsdp"]
    if seq_size == 2 * MEMBERS:
        body = functools.partial(grouped, seq_size, fsdp_size)
    else:
        body = plain
    return jax.shard_map(
        body,
        mesh=mesh,
        in_specs=(P("seq", None), P("seq", "fsdp", None), P("seq", "fsdp", None), P(), P("fsdp")),
        out_specs=P("seq", "fsdp"),
        check_vma=False,
    )
```

```python
import functools

import jax
import jax.numpy as jnp
from jax import lax
from jax.experimental import pallas as pl
from jax.experimental.pallas import tpu as pltpu
from jax.sharding import PartitionSpec as P

MEMBERS = 4
VMEM = 60 * 1024 * 1024
VMEM_SMALL = 16 * 1024 * 1024


def doc_index(positions, doc_ends):
    return jnp.sum((positions[:, None] >= doc_ends[None, :]).astype(jnp.int32), axis=1)


def silu(v):
    return v / (1.0 + jnp.exp(-v))


def params(limit=VMEM):
    return pltpu.CompilerParams(vmem_limit_bytes=limit)


def accumulate(step, ranges, t_refs, w_refs, total, start_refs):
    edges, at = [], 0
    for ref in t_refs:
        edges.append((at, at + ref.shape[0]))
        at += ref.shape[0]

    @pl.when(step == 0)
    def _():
        at = 0
        for ref in start_refs:
            total[at : at + ref.shape[0], :] = ref[...]
            at += ref.shape[0]
        if at < total.shape[0]:
            total[at:, :] = jnp.zeros((total.shape[0] - at, total.shape[1]), jnp.float32)

    def run(w_ref, low, high):
        chosen = [r[...] for r, (a, b) in zip(t_refs, edges) if low <= a and b <= high]
        lhs = jnp.concatenate(chosen, axis=0) if len(chosen) > 1 else chosen[0]
        total[low:high, :] += jnp.dot(lhs, w_ref[...], preferred_element_type=jnp.float32)

    for w_ref, (first, end, low, high) in zip(w_refs, ranges):
        pl.when((step >= first) & (step < end))(functools.partial(run, w_ref, low, high))


def project_body(ranges, starts, *refs):
    k_ref, refs = refs[0], refs[1:]
    arrays = len(ranges)
    parts = len(refs) - arrays - starts - 1
    t_refs, w_refs, refs = refs[:parts], refs[parts : parts + arrays], refs[parts + arrays :]
    accumulate(pl.program_id(0), ranges, t_refs, w_refs, refs[-1], refs[:starts])


def settle(places, fsdp_size, where_ref, t_refs, total, out_ref):
    m, f = where_ref[0], where_ref[1]
    block_rows = out_ref.shape[0] // MEMBERS
    at = 0
    for ref, (j, spots) in zip(t_refs, places):
        rows = ref.shape[0] // len(spots)
        for e, offset in spots:
            to = (m ^ j) * block_rows
            if e is not None:
                to = to + (f ^ e) * (block_rows // fsdp_size) + offset
            to = pl.multiple_of(to, 16)
            out_ref[pl.ds(to, rows), :] = silu(total[at : at + rows, :]).astype(out_ref.dtype)
            at += rows


def activate_body(places, fsdp_size, ranges, starts, where_ref, k_ref, *refs):
    parts, arrays = len(places), len(ranges)
    t_refs, w_refs, refs = refs[:parts], refs[parts : parts + arrays], refs[parts + arrays :]
    start_refs, out_ref, total = refs[:starts], refs[-2], refs[-1]
    step = pl.program_id(0)
    accumulate(step, ranges, t_refs, w_refs, total, start_refs)

    @pl.when(step == ranges[-1][1] - 1)
    def _():
        settle(places, fsdp_size, where_ref, t_refs, total, out_ref)


def keyval_body(places, fsdp_size, ranges, starts, heads, where_ref, k_ref, ends_ref, *refs):
    parts, arrays = len(places), len(ranges)
    t_refs, w_refs, refs = refs[:parts], refs[parts : parts + arrays], refs[parts + arrays :]
    start_refs, (out_ref, tails_ref, state_ref, total) = refs[:starts], refs[starts:]
    step = pl.program_id(0)
    accumulate(step, ranges, t_refs, w_refs, total, start_refs)

    @pl.when(step == ranges[-1][1] - 1)
    def _():
        settle(places, fsdp_size, where_ref, t_refs, total, out_ref)
        rows = out_ref.shape[0] // MEMBERS
        size = out_ref.shape[1] // heads // 2
        for b in range(MEMBERS):
            start = (where_ref[2] * MEMBERS + b) * rows
            last = doc_of_scalar(start + rows - 1, ends_ref)
            before = doc_of_scalar(start - 1, ends_ref)
            docs = doc_of(start + lax.broadcasted_iota(jnp.int32, (rows, 1), 0), ends_ref)
            mask = docs == last
            kept = jnp.where(before == last, 1.0, 0.0)
            for h in range(heads):
                at = 2 * h * size
                keys = out_ref[b * rows : (b + 1) * rows, at : at + size]
                keys = jnp.where(mask, keys.astype(jnp.float32), 0.0).astype(keys.dtype)
                values = out_ref[b * rows : (b + 1) * rows, at + size : at + 2 * size]
                tail = lax.dot_general(
                    keys, values, (((0,), (0,)), ((), ())), preferred_element_type=jnp.float32
                )
                tails_ref[b, h] = tail
                state_ref[h] = tail + kept * state_ref[h] if b else tail


def part_rows(part, depth):
    return part.shape[0] * part.shape[1] // (depth * lax.axis_size("seq"))


def part_spec(part, depth, block):
    if part.shape[1] == depth:
        return pl.BlockSpec((part_rows(part, depth), depth), lambda *a: (block(*a), 0))
    return pl.BlockSpec((part.shape[0], depth), lambda *a: (0, block(*a)))


def project(where, k_blocks, parts, weights, depth, column, width, starts=(), kind="sum", ends=None):
    counts = [part_rows(p, depth) for p, _ in parts]
    rows = sum(counts)
    ranges, spans, steps = [], [None] * len(parts), 0
    for w, a, b in weights:
        end = steps + w.shape[0] // depth
        ranges.append((steps, end, sum(counts[:a]), sum(counts[:b])))
        for i in range(a, b):
            spans[i] = (spans[i][0] if spans[i] else steps, end)
        steps = end
    in_specs = [
        part_spec(p, depth, lambda k, kb, *_, s=s: kb[jnp.clip(k, s[0], s[1] - 1)])
        for (p, _), s in zip(parts, spans)
    ]
    in_specs += [
        pl.BlockSpec(
            (depth, width),
            lambda k, *_, r=r, c=column if w.shape[1] > width else 0: (
                jnp.clip(k - r[0], 0, r[1] - r[0] - 1),
                c,
            ),
        )
        for (w, _, _), r in zip(weights, ranges)
    ]
    in_specs += [
        pl.BlockSpec((count, width), lambda k, *_, at=at, c=c: (at, c)) for _, at, count, c in starts
    ]
    operands = [p for p, _ in parts] + [w for w, _, _ in weights] + [a for a, _, _, _ in starts]
    whole = pl.BlockSpec((rows, width), lambda k, *_: (0, 0))
    scratch = [pltpu.VMEM((rows, width), jnp.float32)]
    places, fsdp_size = [p for _, p in parts], lax.axis_size("fsdp")
    if kind == "sum":
        prefetch, scratch = [k_blocks], []
        body = functools.partial(project_body, ranges, len(starts))
        out_specs, out_shape = whole, jax.ShapeDtypeStruct((rows, width), jnp.float32)
    elif kind == "query":
        prefetch = [where, k_blocks]
        body = functools.partial(activate_body, places, fsdp_size, ranges, len(starts))
        out_specs, out_shape = whole, jax.ShapeDtypeStruct((rows, width), jnp.bfloat16)
    else:
        heads, size = kind
        prefetch = [where, k_blocks, ends]
        body = functools.partial(keyval_body, places, fsdp_size, ranges, len(starts), heads)
        out_specs = [
            whole,
            pl.BlockSpec((MEMBERS, heads, size, size), lambda k, *_: (0, 0, 0, 0)),
            pl.BlockSpec((heads, size, size), lambda k, *_: (0, 0, 0)),
        ]
        out_shape = [
            jax.ShapeDtypeStruct((rows, width), jnp.bfloat16),
            jax.ShapeDtypeStruct((MEMBERS, heads, size, size), jnp.float32),
            jax.ShapeDtypeStruct((heads, size, size), jnp.float32),
        ]
    at = prefetch.index(k_blocks) if kind == "sum" else 1
    if at:
        for i, p in enumerate(parts):
            s = spans[i]
            in_specs[i] = part_spec(
                p[0], depth, lambda k, wh, kb, *_, s=s: kb[jnp.clip(k, s[0], s[1] - 1)]
            )
    work = sum((r[1] - r[0]) * (r[3] - r[2]) for r in ranges)
    return pl.pallas_call(
        body,
        grid_spec=pltpu.PrefetchScalarGridSpec(
            num_scalar_prefetch=len(prefetch),
            grid=(steps,),
            in_specs=in_specs,
            out_specs=out_specs,
            scratch_shapes=scratch,
        ),
        out_shape=out_shape,
        compiler_params=params(),
        cost_estimate=pl.CostEstimate(
            flops=2 * work * depth * width,
            bytes_accessed=2 * depth * (work + steps * width) + 8 * rows * width,
            transcendentals=0,
        ),
    )(*prefetch, *operands)


def doc_of(positions, ends_ref):
    total = jnp.zeros(positions.shape, jnp.int32)
    for i in range(ends_ref.shape[0]):
        total += (positions >= ends_ref[i]).astype(jnp.int32)
    return total


def doc_of_scalar(position, ends_ref):
    total = jnp.int32(0)
    for i in range(ends_ref.shape[0]):
        total += (position >= ends_ref[i]).astype(jnp.int32)
    return total


def attend_body(place, cut, where_ref, ends_ref, q_ref, kv_ref, tails_ref, other_ref, out_ref, square_ref):
    rows, width = q_ref.shape
    heads, size = other_ref.shape[0], other_ref.shape[1]
    m, g = where_ref[0], where_ref[2]
    block = m ^ place
    origin = g * MEMBERS * rows
    start = origin + block * rows
    before = doc_of_scalar(start - 1, ends_ref)

    edge = doc_of_scalar(origin - 1, ends_ref)
    owner = doc_of_scalar(((g ^ 1) + 1) * MEMBERS * rows - 1, ends_ref)
    state = jnp.where((g == 1) & (owner == edge), 1.0, 0.0) * other_ref[...]
    for i in range(MEMBERS - 1):
        prior = doc_of_scalar(origin + i * rows - 1, ends_ref)
        ended = doc_of_scalar(origin + (i + 1) * rows - 1, ends_ref)
        follows = tails_ref[i] + jnp.where(prior == ended, 1.0, 0.0) * state
        state = jnp.where(i < block, follows, state)
    incoming = state.astype(jnp.bfloat16)

    row_docs = doc_of(start + lax.broadcasted_iota(jnp.int32, (1, rows), 1), ends_ref)
    for begin in range(0, rows, cut):
        seen = begin + cut
        docs = doc_of(start + begin + lax.broadcasted_iota(jnp.int32, (cut, 1), 0), ends_ref)
        at = begin + lax.broadcasted_iota(jnp.int32, (cut, seen), 0)
        behind = lax.broadcasted_iota(jnp.int32, (cut, seen), 1)
        mask = (at >= behind) & (docs == row_docs[:, :seen])
        mixed = []
        for h in range(heads):
            k_at, v_at = 2 * h * size, (2 * h + 1) * size
            q = q_ref[begin:seen, h * size : (h + 1) * size]
            scores = lax.dot_general(
                q, kv_ref[:seen, k_at : k_at + size], (((1,), (1,)), ((), ())),
                preferred_element_type=jnp.float32,
            )
            weights = jnp.where(mask, scores, 0.0).astype(jnp.bfloat16)
            within = jnp.dot(
                weights, kv_ref[:seen, v_at : v_at + size], preferred_element_type=jnp.float32
            )
            carried = jnp.dot(q, incoming[h], preferred_element_type=jnp.float32)
            mixed.append(within + jnp.where(docs == before, carried, 0.0))
        mixed = jnp.concatenate(mixed, axis=1)
        out_ref[begin:seen, :] = mixed.astype(out_ref.dtype)
        sums = lax.dot_general(
            jnp.ones((8, width), jnp.float32), mixed * mixed, (((1,), (1,)), ((), ())),
            preferred_element_type=jnp.float32,
        )
        square_ref[:, begin:seen] = sums[:1]


def attend(where, ends, place, q, kv, tail, other):
    rows, width = q.shape[0] // MEMBERS, q.shape[1]
    heads, size = other.shape[0], other.shape[1]
    cut = rows // 3 if rows % 384 == 0 else rows
    return pl.pallas_call(
        functools.partial(attend_body, place, cut),
        grid_spec=pltpu.PrefetchScalarGridSpec(
            num_scalar_prefetch=2,
            grid=(1,),
            in_specs=[
                pl.BlockSpec((rows, width), lambda i, wh, en: (wh[0] ^ place, 0)),
                pl.BlockSpec((rows, kv.shape[1]), lambda i, wh, en: (wh[0] ^ place, 0)),
                pl.BlockSpec(tail.shape, lambda i, wh, en: (0, 0, 0, 0)),
                pl.BlockSpec(other.shape, lambda i, wh, en: (0, 0, 0)),
            ],
            out_specs=[
                pl.BlockSpec((rows, width), lambda i, wh, en: (0, 0)),
                pl.BlockSpec((1, rows), lambda i, wh, en: (0, 0)),
            ],
        ),
        out_shape=[
            jax.ShapeDtypeStruct((rows, width), jnp.bfloat16),
            jax.ShapeDtypeStruct((1, rows), jnp.float32),
        ],
        compiler_params=params(VMEM_SMALL),
        cost_estimate=pl.CostEstimate(
            flops=3 * rows * rows * width + 2 * rows * width * size,
            bytes_accessed=8 * rows * width,
            transcendentals=0,
        ),
    )(where, ends, q, kv, tail, other)


def finish_body(count, where_ref, *refs):
    squares_ref, gain_ref, out_ref = refs[MEMBERS:]
    rows, width = refs[0].shape
    inverse = lax.rsqrt(squares_ref[...] / count + 1e-06)
    inverse = jnp.transpose(jnp.broadcast_to(inverse, (128, rows)))[:, :1]
    for k in range(MEMBERS):
        at = pl.multiple_of((where_ref[0] ^ k) * width, width)
        gain = gain_ref[:, pl.ds(at, width)].astype(jnp.float32)
        value = refs[k][...].astype(jnp.float32) * inverse * gain
        out_ref[:, pl.ds(at, width)] = value.astype(out_ref.dtype)


def finish(where, parts, squares, gain, count):
    rows, width = parts[0].shape
    cut = rows // 3 if rows % 384 == 0 else rows
    return pl.pallas_call(
        functools.partial(finish_body, count),
        grid_spec=pltpu.PrefetchScalarGridSpec(
            num_scalar_prefetch=1,
            grid=(rows // cut,),
            in_specs=[pl.BlockSpec((cut, width), lambda i, wh: (i, 0)) for _ in parts]
            + [
                pl.BlockSpec((1, cut), lambda i, wh: (0, i)),
                pl.BlockSpec((1, MEMBERS * width), lambda i, wh: (0, 0)),
            ],
            out_specs=pl.BlockSpec((cut, MEMBERS * width), lambda i, wh: (i, 0)),
        ),
        out_shape=jax.ShapeDtypeStruct((rows, MEMBERS * width), jnp.bfloat16),
        compiler_params=params(VMEM_SMALL),
    )(where, *parts, squares, gain)


def grouped(seq_size, fsdp_size, tokens, w_query, w_keyval, doc_lengths, norm_gain):
    rows, model = tokens.shape
    depth, head_count, size = w_query.shape
    heads = head_count // MEMBERS
    s = lax.axis_index("seq")
    f = lax.axis_index("fsdp")
    m = lax.rem(s, MEMBERS)
    g = lax.div(s, MEMBERS)
    where = jnp.stack([m, f, g]).astype(jnp.int32)
    doc_ends = jnp.cumsum(doc_lengths)

    inner = ((s >> 1) ^ (s >> 2)) & 1 == 1
    inner_seq = [i for i in range(seq_size) if ((i >> 1) ^ (i >> 2)) & 1 == 1]
    outer_seq = [i for i in range(seq_size) if i not in inner_seq]

    def hop(value, k, only=range(seq_size)):
        return lax.ppermute(value, "seq", [(i, i ^ k) for i in only])

    def side(value, k):
        return lax.ppermute(value, "fsdp", [(i, i ^ k) for i in range(fsdp_size)])

    q_width, kv_width = heads * size, 2 * heads * size
    width = kv_width + q_width
    q_block = kv_width // q_width
    flat_kv = w_keyval.reshape(depth, head_count * 2 * size)
    flat_q = w_query.reshape(depth, head_count * size)

    def columns(k):
        at = m ^ k
        return jnp.concatenate(
            [
                lax.dynamic_slice(flat_kv, (0, at * kv_width), (depth, kv_width)),
                lax.dynamic_slice(flat_q, (0, at * q_width), (depth, q_width)),
            ],
            axis=1,
        )

    half = rows // fsdp_size // 2

    def own(i):
        chunk = lax.dynamic_slice(tokens, ((2 * f + i) * half, 0), (half, model))
        return chunk.reshape(half, seq_size, depth).transpose(1, 0, 2).reshape(-1, depth)

    history = [[], []]

    def stage(extra, ops, ties="chain"):
        found, before = [], history[-1]
        for chain, move, operand in ops:
            waits = list(extra)
            if ties == "chain":
                waits += [v for _, v in history[-2]] + [v for c_, v in before if c_ == chain]
            elif ties == "all":
                waits += [v for _, v in before]
            if waits:
                operand = lax.optimization_barrier((operand, tuple(waits)))[0]
            found.append((chain, move(operand)))
        history.append(found)
        return [v for _, v in found]

    def blocks(ks):
        return jnp.stack([s ^ k for k in ks]).astype(jnp.int32)

    def pairs(inner_hop, outer_hop):
        moves = [(i, i ^ inner_hop) for i in inner_seq if inner_hop]
        moves += [(i, i ^ outer_hop) for i in outer_seq if outer_hop]
        return lambda value: lax.ppermute(value, "seq", moves)

    def pick(a, b):
        return jnp.where(inner, a, b)

    def spread(j, first, second):
        found = []
        for offset, pieces in ((0, first), (half, second)):
            found += [(p, (j, [(e, offset)])) for e, p in zip((0, 2, 1, 3), pieces)]
        return found

    def x(value):
        return hop(value, 1)

    def y(value):
        return side(value, 2)

    def c(value):
        return side(value, 1)

    both_ways = pairs(2, 2)
    part0 = [(tokens, (0, [(None, 0)]))]
    own1 = own(0)
    wb = columns(2)
    r1, tz1, tx1 = stage([], [("z", pairs(6, 0), wb), ("z", both_ways, own1), ("x", x, own1)])
    wa, wc, wd, own2 = columns(0), columns(1), columns(3), own(1)
    in2, in3 = pick(wa, own2), pick(own2, wa)
    x_first, x_second = pick(wd, wc), pick(wc, wd)
    r2, tx2, yx1, cx1, cz1 = stage(
        [x_first, x_second, own2, in2, in3],
        [("z", pairs(4, 2), in2), ("x", x, own2), ("y", y, tx1), ("c", c, tx1), ("c", c, tz1)],
    )
    r3, rx1, yx2, cx2, dx1 = stage(
        [], [("z", pairs(2, 4), in3), ("x", x, x_first), ("y", y, tx2), ("c", c, tx2), ("c", c, yx1)]
    )
    r4, tzx1, yz1, dx2 = stage(
        [], [("z", pairs(0, 6), wb), ("x", x, tz1), ("y", y, tz1), ("c", c, yx2)]
    )
    tz2, w4 = pick(r2, r3), pick(r3, r2)
    rx1_kv, rx1_q = rx1[:, :kv_width], rx1[:, kv_width:]
    part1 = spread(1, (tx1, yx1, cx1, dx1), (tx2, yx2, cx2, dx2))
    r5, z5, rx2, yzx1, dz1 = stage(
        [tz2, w4, rx1_kv, rx1_q],
        [("z", pairs(6, 0), rx1), ("z", both_ways, wb), ("x", x, x_second), ("y", y, tzx1), ("c", c, yz1)],
    )
    w6 = pick(r1, r4)
    near = part0 + part1
    n = len(near)
    acc_a = project(
        where, blocks([0, 4, 6]), near, [(w, 0, n) for w in (wa, w4, w6)], depth, 0, width
    )
    r6, tzx2, yz2, czx1, dzx1 = stage(
        [acc_a],
        [("z", pairs(4, 2), rx2), ("x", x, tz2), ("y", y, tz2), ("c", c, tzx1), ("c", c, yzx1)],
    )
    rx2_kv, rx2_q = rx2[:, :kv_width], rx2[:, kv_width:]
    rxa = pick(rx2, rx1)
    five, w_five = [0, 4, 6, 1, 2], [wa, w4, w6, rxa, z5]
    first2 = spread(2, (tz1, yz1, cz1, dz1), [None] * 4)[:4]
    acc_a = project(
        where, blocks(five), near + first2,
        [(w, n, n + 4) for w in w_five[:3]] + [(w, 0, n + 4) for w in w_five[3:]], depth, 0, width,
        starts=[(acc_a, 0, 2 * rows, 0)],
    )
    r7, yzx2, cz2, czx2, dz2 = stage(
        [acc_a, rx2_kv, rx2_q],
        [("z", pairs(2, 4), rx1_kv), ("y", y, tzx2), ("c", c, tz2), ("c", c, tzx2), ("c", c, yz2)],
        "all",
    )
    sixth = (s ^ pick(3, 5))[None].astype(jnp.int32)
    six = jnp.concatenate([blocks(five), sixth])
    first3 = spread(3, (tzx1, yzx1, czx1, dzx1), [None] * 4)[:4]
    most = near + first2 + first3
    acc_b = project(
        where, six, most, [(w, n + 4, n + 8) for w in w_five] + [(r6, 0, n + 8)], depth, 0, width,
        starts=[(acc_a, 0, 2 * rows + rows // 2, 0)],
    )
    dzx2, r8 = stage([acc_b], [("c", c, yzx2), ("z", pairs(0, 6), rx2_kv)], "all")
    rest = spread(2, [None] * 4, (tz2, yz2, cz2, dz2))[4:]
    rest += spread(3, [None] * 4, (tzx2, yzx2, czx2, dzx2))[4:]
    acc_c = project(where, six, rest, [(w, 0, 8) for w in w_five + [r6]], depth, 0, width)
    r7q, r8q = stage(
        [acc_c], [("z", pairs(2, 4), rx1_q), ("z", pairs(0, 6), rx2_q)], ties=None
    )

    r8 = lax.optimization_barrier((r8, acc_c))[0]
    every = most + rest
    last = jnp.stack([s ^ pick(5, 3), s ^ 7]).astype(jnp.int32)

    def finals(column):
        return [(acc_b, 0, 3 * rows, column), (acc_c, 0, rows, column)]

    keyval, tail, state = project(
        where, last, every, [(w, 0, len(every)) for w in (r7, pick(r5[:, :kv_width], r8))],
        depth, 0, kv_width, starts=finals(0), kind=(heads, size), ends=doc_ends,
    )
    other = hop(state, MEMBERS)
    queries = project(
        where, last, every, [(w, 0, len(every)) for w in (r7q, pick(r5[:, kv_width:], r8q))],
        depth, 0, q_width, starts=finals(q_block), kind="query",
    )

    outs, squares, sent = {}, 0.0, []
    for k in (3, 2, 1, 0):
        if k == 0:
            queries = lax.optimization_barrier((queries, sent[0]))[0]
        outs[k], square = attend(where, doc_ends, k, queries, keyval, tail, other)
        if k:
            outs[k], square = hop(outs[k], k), hop(square, k)
            sent.append(outs[k])
        squares = squares + square
    squares = squares + sum(side(squares, k) for k in range(1, fsdp_size))
    return finish(
        where, [outs[k] for k in range(MEMBERS)], squares, norm_gain[None, :],
        head_count * fsdp_size * size,
    )


def plain(tokens, w_query, w_keyval, doc_lengths, norm_gain):
    rows_here = tokens.shape[0]
    head_count = w_query.shape[1]
    head_size = w_query.shape[2]
    shard_index = lax.axis_index("seq")
    doc_ends = jnp.cumsum(doc_lengths)
    offsets = lax.iota(jnp.int32, rows_here)
    doc_ids = doc_index(shard_index * rows_here + offsets, doc_ends)
    first_doc = doc_ids[0]
    tail_doc = doc_ids[rows_here - 1]

    def project(panel_rows):
        panel = panel_rows.reshape(panel_rows.shape[0], panel_rows.shape[1] * panel_rows.shape[2])
        return jnp.dot(tokens, panel, preferred_element_type=jnp.float32)

    query_sum = project(lax.all_gather(w_query, "seq", axis=0, tiled=True))
    keyval_sum = project(lax.all_gather(w_keyval, "seq", axis=0, tiled=True))
    keyval = (
        jax.nn.silu(keyval_sum).astype(jnp.bfloat16).reshape(rows_here, head_count, 2 * head_size)
    )
    key_rows = keyval[:, :, :head_size]
    values = keyval[:, :, head_size:]
    tail_mask = (doc_ids == tail_doc).astype(jnp.bfloat16)
    tail_state = jnp.einsum(
        "thd,the->hde",
        key_rows * tail_mask[:, None, None],
        values,
        preferred_element_type=jnp.float32,
    )
    states = lax.all_gather(tail_state[None], "seq", axis=0, tiled=True)
    shard_ids = lax.iota(jnp.int32, states.shape[0])
    owner_docs = doc_index(shard_ids * rows_here + rows_here - 1, doc_ends)
    selected = ((shard_ids < shard_index) & (owner_docs == first_doc)).astype(jnp.float32)
    incoming = jnp.sum(selected[:, None, None, None] * states, axis=0)
    queries = jax.nn.silu(query_sum).astype(jnp.bfloat16).reshape(rows_here, head_count, head_size)
    scores = jnp.einsum("thd,shd->hts", queries, key_rows, preferred_element_type=jnp.float32)
    causal = (
        (offsets[:, None] >= offsets[None, :]) & (doc_ids[:, None] == doc_ids[None, :])
    ).astype(jnp.float32)
    weights = (scores * causal[None]).astype(jnp.bfloat16)
    within = jnp.einsum("hts,she->the", weights, values, preferred_element_type=jnp.float32)
    carried = jnp.einsum(
        "thd,hde->the", queries, incoming.astype(jnp.bfloat16), preferred_element_type=jnp.float32
    )
    carried = carried * (doc_ids == first_doc).astype(jnp.float32)[:, None, None]
    mixed = within + carried
    sum_squares = lax.psum(jnp.sum(mixed * mixed, axis=(1, 2)), "fsdp")
    inverse_rms = lax.rsqrt(sum_squares / (head_count * lax.axis_size("fsdp") * head_size) + 1e-06)
    flat = mixed.reshape(rows_here, head_count * head_size)
    return (flat * inverse_rms[:, None] * norm_gain.astype(jnp.float32)[None, :]).astype(
        jnp.bfloat16
    )


def solution(mesh):
    seq_size, fsdp_size = mesh.shape["seq"], mesh.shape["fsdp"]
    if seq_size == 2 * MEMBERS:
        body = functools.partial(grouped, seq_size, fsdp_size)
    else:
        body = plain
    return jax.shard_map(
        body,
        mesh=mesh,
        in_specs=(P("seq", None), P("seq", "fsdp", None), P("seq", "fsdp", None), P(), P("fsdp")),
        out_specs=P("seq", "fsdp"),
        check_vma=False,
    )
```

```python
import functools

import jax
import jax.numpy as jnp
from jax import lax
from jax.experimental import pallas as pl
from jax.experimental.pallas import tpu as pltpu
from jax.sharding import PartitionSpec as P

MEMBERS = 4
VMEM = 60 * 1024 * 1024
VMEM_SMALL = 16 * 1024 * 1024


def doc_index(positions, doc_ends):
    return jnp.sum((positions[:, None] >= doc_ends[None, :]).astype(jnp.int32), axis=1)


def silu(v):
    return v / (1.0 + jnp.exp(-v))


def params(limit=VMEM):
    return pltpu.CompilerParams(vmem_limit_bytes=limit)


def accumulate(step, ranges, t_refs, w_refs, total, start_refs, inner=None):
    edges, at = [], 0
    for ref in t_refs:
        edges.append((at, at + ref.shape[0]))
        at += ref.shape[0]

    @pl.when(step == 0)
    def _():
        at = 0
        for ref in start_refs:
            total[at : at + ref.shape[0], :] = ref[...]
            at += ref.shape[0]
        if at < total.shape[0]:
            total[at:, :] = jnp.zeros((total.shape[0] - at, total.shape[1]), jnp.float32)

    def run(w_ref, low, high):
        chosen = [r[...] for r, (a, b) in zip(t_refs, edges) if low <= a and b <= high]
        lhs = jnp.concatenate(chosen, axis=0) if len(chosen) > 1 else chosen[0]
        total[low:high, :] += jnp.dot(lhs, w_ref[...], preferred_element_type=jnp.float32)

    for w_ref, (first, end, low, high, place) in zip(w_refs, ranges):
        here = (step >= first) & (step < end)
        if place is not None:
            here = here & (inner == place)
        pl.when(here)(functools.partial(run, w_ref, low, high))


def project_body(ranges, starts, *refs):
    k_ref, refs = refs[0], refs[1:]
    arrays = len(ranges)
    parts = len(refs) - arrays - starts - 1
    t_refs, w_refs, refs = refs[:parts], refs[parts : parts + arrays], refs[parts + arrays :]
    accumulate(pl.program_id(0), ranges, t_refs, w_refs, refs[-1], refs[:starts])


def settle(places, fsdp_size, where_ref, t_refs, total, out_ref):
    m, f = where_ref[0], where_ref[1]
    block_rows = out_ref.shape[0] // MEMBERS
    at = 0
    for ref, (j, spots) in zip(t_refs, places):
        rows = ref.shape[0] // len(spots)
        for e, offset in spots:
            to = (m ^ j) * block_rows
            if e is not None:
                to = to + (f ^ e) * (block_rows // fsdp_size) + offset
            to = pl.multiple_of(to, 16)
            out_ref[pl.ds(to, rows), :] = silu(total[at : at + rows, :]).astype(out_ref.dtype)
            at += rows


def activate_body(places, fsdp_size, ranges, starts, where_ref, k_ref, *refs):
    parts, arrays = len(places), len(ranges)
    t_refs, w_refs, refs = refs[:parts], refs[parts : parts + arrays], refs[parts + arrays :]
    start_refs, out_ref, total = refs[:starts], refs[-2], refs[-1]
    step = pl.program_id(0)
    accumulate(step, ranges, t_refs, w_refs, total, start_refs, where_ref[3])

    @pl.when(step == ranges[-1][1] - 1)
    def _():
        settle(places, fsdp_size, where_ref, t_refs, total, out_ref)


def keyval_body(places, fsdp_size, ranges, starts, heads, where_ref, k_ref, ends_ref, *refs):
    parts, arrays = len(places), len(ranges)
    t_refs, w_refs, refs = refs[:parts], refs[parts : parts + arrays], refs[parts + arrays :]
    start_refs, (out_ref, tails_ref, state_ref, total) = refs[:starts], refs[starts:]
    step = pl.program_id(0)
    accumulate(step, ranges, t_refs, w_refs, total, start_refs, where_ref[3])

    @pl.when(step == ranges[-1][1] - 1)
    def _():
        settle(places, fsdp_size, where_ref, t_refs, total, out_ref)
        rows = out_ref.shape[0] // MEMBERS
        size = out_ref.shape[1] // heads // 2
        for b in range(MEMBERS):
            start = (where_ref[2] * MEMBERS + b) * rows
            last = doc_of_scalar(start + rows - 1, ends_ref)
            before = doc_of_scalar(start - 1, ends_ref)
            docs = doc_of(start + lax.broadcasted_iota(jnp.int32, (rows, 1), 0), ends_ref)
            mask = docs == last
            kept = jnp.where(before == last, 1.0, 0.0)
            for h in range(heads):
                at = 2 * h * size
                keys = out_ref[b * rows : (b + 1) * rows, at : at + size]
                keys = jnp.where(mask, keys.astype(jnp.float32), 0.0).astype(keys.dtype)
                values = out_ref[b * rows : (b + 1) * rows, at + size : at + 2 * size]
                tail = lax.dot_general(
                    keys, values, (((0,), (0,)), ((), ())), preferred_element_type=jnp.float32
                )
                tails_ref[b, h] = tail
                state_ref[h] = tail + kept * state_ref[h] if b else tail


def part_rows(part, depth):
    return part.shape[-2] * part.shape[-1] // (depth * lax.axis_size("seq"))


def part_spec(part, depth, block):
    if part.shape[1] == depth:
        return pl.BlockSpec((part_rows(part, depth), depth), lambda *a: (block(*a), 0))
    return pl.BlockSpec((part.shape[0], depth), lambda *a: (0, block(*a)))


def project(where, k_blocks, parts, weights, depth, column, width, starts=(), kind="sum", ends=None):
    counts = [part_rows(p, depth) for p, _ in parts]
    rows = sum(counts)
    ranges, spans, steps = [], [None] * len(parts), 0
    arrays = []
    for w, a, b in weights:
        choices = w if isinstance(w, tuple) else (w,)
        end = steps + choices[0].shape[0] // depth
        for place, choice in enumerate(choices):
            place = place if len(choices) > 1 else None
            ranges.append((steps, end, sum(counts[:a]), sum(counts[:b]), place))
            arrays.append(choice)
        for i in range(a, b):
            spans[i] = (spans[i][0] if spans[i] else steps, end)
        steps = end
    in_specs = [
        part_spec(p, depth, lambda k, kb, *_, s=s: kb[jnp.clip(k, s[0], s[1] - 1)])
        for (p, _), s in zip(parts, spans)
    ]
    in_specs += [
        pl.BlockSpec(
            (depth, width),
            lambda k, *_, r=r, c=column if w.shape[1] > width else 0: (
                jnp.clip(k - r[0], 0, r[1] - r[0] - 1),
                c,
            ),
        )
        for w, r in zip(arrays, ranges)
    ]
    in_specs += [
        pl.BlockSpec((count, width), lambda k, *_, at=at, c=c: (at, c)) for _, at, count, c in starts
    ]
    operands = [p for p, _ in parts] + arrays + [a for a, _, _, _ in starts]
    whole = pl.BlockSpec((rows, width), lambda k, *_: (0, 0))
    scratch = [pltpu.VMEM((rows, width), jnp.float32)]
    places, fsdp_size = [p for _, p in parts], lax.axis_size("fsdp")
    if kind == "sum":
        prefetch, scratch = [k_blocks], []
        body = functools.partial(project_body, ranges, len(starts))
        out_specs, out_shape = whole, jax.ShapeDtypeStruct((rows, width), jnp.float32)
    elif kind == "query":
        prefetch = [where, k_blocks]
        body = functools.partial(activate_body, places, fsdp_size, ranges, len(starts))
        out_specs, out_shape = whole, jax.ShapeDtypeStruct((rows, width), jnp.bfloat16)
    else:
        heads, size = kind
        prefetch = [where, k_blocks, ends]
        body = functools.partial(keyval_body, places, fsdp_size, ranges, len(starts), heads)
        out_specs = [
            whole,
            pl.BlockSpec((MEMBERS, heads, size, size), lambda k, *_: (0, 0, 0, 0)),
            pl.BlockSpec((heads, size, size), lambda k, *_: (0, 0, 0)),
        ]
        out_shape = [
            jax.ShapeDtypeStruct((rows, width), jnp.bfloat16),
            jax.ShapeDtypeStruct((MEMBERS, heads, size, size), jnp.float32),
            jax.ShapeDtypeStruct((heads, size, size), jnp.float32),
        ]
    at = prefetch.index(k_blocks) if kind == "sum" else 1
    if at:
        for i, p in enumerate(parts):
            s = spans[i]
            in_specs[i] = part_spec(
                p[0], depth, lambda k, wh, kb, *_, s=s: kb[jnp.clip(k, s[0], s[1] - 1)]
            )
    work = sum((r[1] - r[0]) * (r[3] - r[2]) for r in ranges)
    return pl.pallas_call(
        body,
        grid_spec=pltpu.PrefetchScalarGridSpec(
            num_scalar_prefetch=len(prefetch),
            grid=(steps,),
            in_specs=in_specs,
            out_specs=out_specs,
            scratch_shapes=scratch,
        ),
        out_shape=out_shape,
        compiler_params=params(),
        cost_estimate=pl.CostEstimate(
            flops=2 * work * depth * width,
            bytes_accessed=2 * depth * (work + steps * width) + 8 * rows * width,
            transcendentals=0,
        ),
    )(*prefetch, *operands)


def doc_of(positions, ends_ref):
    total = jnp.zeros(positions.shape, jnp.int32)
    for i in range(ends_ref.shape[0]):
        total += (positions >= ends_ref[i]).astype(jnp.int32)
    return total


def doc_of_scalar(position, ends_ref):
    total = jnp.int32(0)
    for i in range(ends_ref.shape[0]):
        total += (position >= ends_ref[i]).astype(jnp.int32)
    return total


def attend_body(place, cut, where_ref, ends_ref, q_ref, kv_ref, tails_ref, other_ref, out_ref, square_ref):
    rows, width = q_ref.shape
    heads, size = other_ref.shape[0], other_ref.shape[1]
    m, g = where_ref[0], where_ref[2]
    block = m ^ place
    origin = g * MEMBERS * rows
    start = origin + block * rows
    before = doc_of_scalar(start - 1, ends_ref)

    edge = doc_of_scalar(origin - 1, ends_ref)
    owner = doc_of_scalar(((g ^ 1) + 1) * MEMBERS * rows - 1, ends_ref)
    state = jnp.where((g == 1) & (owner == edge), 1.0, 0.0) * other_ref[...]
    for i in range(MEMBERS - 1):
        prior = doc_of_scalar(origin + i * rows - 1, ends_ref)
        ended = doc_of_scalar(origin + (i + 1) * rows - 1, ends_ref)
        follows = tails_ref[i] + jnp.where(prior == ended, 1.0, 0.0) * state
        state = jnp.where(i < block, follows, state)
    incoming = state.astype(jnp.bfloat16)

    row_docs = doc_of(start + lax.broadcasted_iota(jnp.int32, (1, rows), 1), ends_ref)
    for begin in range(0, rows, cut):
        seen = begin + cut
        docs = doc_of(start + begin + lax.broadcasted_iota(jnp.int32, (cut, 1), 0), ends_ref)
        at = begin + lax.broadcasted_iota(jnp.int32, (cut, seen), 0)
        behind = lax.broadcasted_iota(jnp.int32, (cut, seen), 1)
        mask = (at >= behind) & (docs == row_docs[:, :seen])
        mixed = []
        for h in range(heads):
            k_at, v_at = 2 * h * size, (2 * h + 1) * size
            q = q_ref[begin:seen, h * size : (h + 1) * size]
            scores = lax.dot_general(
                q, kv_ref[:seen, k_at : k_at + size], (((1,), (1,)), ((), ())),
                preferred_element_type=jnp.float32,
            )
            weights = jnp.where(mask, scores, 0.0).astype(jnp.bfloat16)
            within = jnp.dot(
                weights, kv_ref[:seen, v_at : v_at + size], preferred_element_type=jnp.float32
            )
            carried = jnp.dot(q, incoming[h], preferred_element_type=jnp.float32)
            mixed.append(within + jnp.where(docs == before, carried, 0.0))
        mixed = jnp.concatenate(mixed, axis=1)
        out_ref[begin:seen, :] = mixed.astype(out_ref.dtype)
        sums = lax.dot_general(
            jnp.ones((8, width), jnp.float32), mixed * mixed, (((1,), (1,)), ((), ())),
            preferred_element_type=jnp.float32,
        )
        square_ref[:, begin:seen] = sums[:1]


def attend(where, ends, place, q, kv, tail, other):
    rows, width = q.shape[0] // MEMBERS, q.shape[1]
    heads, size = other.shape[0], other.shape[1]
    cut = rows // 3 if rows % 384 == 0 else rows
    return pl.pallas_call(
        functools.partial(attend_body, place, cut),
        grid_spec=pltpu.PrefetchScalarGridSpec(
            num_scalar_prefetch=2,
            grid=(1,),
            in_specs=[
                pl.BlockSpec((rows, width), lambda i, wh, en: (wh[0] ^ place, 0)),
                pl.BlockSpec((rows, kv.shape[1]), lambda i, wh, en: (wh[0] ^ place, 0)),
                pl.BlockSpec(tail.shape, lambda i, wh, en: (0, 0, 0, 0)),
                pl.BlockSpec(other.shape, lambda i, wh, en: (0, 0, 0)),
            ],
            out_specs=[
                pl.BlockSpec((rows, width), lambda i, wh, en: (0, 0)),
                pl.BlockSpec((1, rows), lambda i, wh, en: (0, 0)),
            ],
        ),
        out_shape=[
            jax.ShapeDtypeStruct((rows, width), jnp.bfloat16),
            jax.ShapeDtypeStruct((1, rows), jnp.float32),
        ],
        compiler_params=params(VMEM_SMALL),
        cost_estimate=pl.CostEstimate(
            flops=3 * rows * rows * width + 2 * rows * width * size,
            bytes_accessed=8 * rows * width,
            transcendentals=0,
        ),
    )(where, ends, q, kv, tail, other)


def finish_body(count, where_ref, *refs):
    squares_ref, gain_ref, out_ref = refs[MEMBERS:]
    rows, width = refs[0].shape
    inverse = lax.rsqrt(squares_ref[...] / count + 1e-06)
    inverse = jnp.transpose(jnp.broadcast_to(inverse, (128, rows)))[:, :1]
    for k in range(MEMBERS):
        at = pl.multiple_of((where_ref[0] ^ k) * width, width)
        gain = gain_ref[:, pl.ds(at, width)].astype(jnp.float32)
        value = refs[k][...].astype(jnp.float32) * inverse * gain
        out_ref[:, pl.ds(at, width)] = value.astype(out_ref.dtype)


def finish(where, parts, squares, gain, count):
    rows, width = parts[0].shape
    cut = rows // 3 if rows % 384 == 0 else rows
    return pl.pallas_call(
        functools.partial(finish_body, count),
        grid_spec=pltpu.PrefetchScalarGridSpec(
            num_scalar_prefetch=1,
            grid=(rows // cut,),
            in_specs=[pl.BlockSpec((cut, width), lambda i, wh: (i, 0)) for _ in parts]
            + [
                pl.BlockSpec((1, cut), lambda i, wh: (0, i)),
                pl.BlockSpec((1, MEMBERS * width), lambda i, wh: (0, 0)),
            ],
            out_specs=pl.BlockSpec((cut, MEMBERS * width), lambda i, wh: (i, 0)),
        ),
        out_shape=jax.ShapeDtypeStruct((rows, MEMBERS * width), jnp.bfloat16),
        compiler_params=params(VMEM_SMALL),
    )(where, *parts, squares, gain)


def stack_columns(out_ref, in_ref):
    rows, depth = in_ref.shape[0], out_ref.shape[1]
    for k in range(out_ref.shape[0] // rows):
        out_ref[k * rows : (k + 1) * rows, :] = in_ref[:, k * depth : (k + 1) * depth]


def stacked_body(where_ref, in_ref, out_ref):
    stack_columns(out_ref, in_ref)


def stacked(where, tokens, rows, depth):
    model = tokens.shape[1]
    return pl.pallas_call(
        stacked_body,
        grid_spec=pltpu.PrefetchScalarGridSpec(
            num_scalar_prefetch=1,
            grid=(1,),
            in_specs=[pl.BlockSpec((rows, model), lambda i, wh: (2 * wh[1], 0))],
            out_specs=pl.BlockSpec((model // depth * rows, depth), lambda i, wh: (0, 0)),
        ),
        out_shape=jax.ShapeDtypeStruct((model // depth * rows, depth), tokens.dtype),
        compiler_params=params(),
    )(where, tokens)


def pack_body(where_ref, kv_ref, q_ref, tokens_ref, a_ref, b_ref, x1_ref, x2_ref, own_ref, in2_ref, in3_ref):
    m, inner = where_ref[0], where_ref[3]
    width = a_ref.shape[1]
    q_width = q_ref.shape[1] // MEMBERS
    kv_width = width - q_width

    def put(ref, member):
        at = pl.multiple_of(member * kv_width, 128)
        ref[:, :kv_width] = kv_ref[:, pl.ds(at, kv_width)]
        at = pl.multiple_of(member * q_width, 128)
        ref[:, kv_width:] = q_ref[:, pl.ds(at, q_width)]

    put(a_ref, m)
    put(b_ref, m ^ 2)
    put(x1_ref, m ^ (1 + 2 * inner))
    put(x2_ref, m ^ (3 - 2 * inner))
    stack_columns(own_ref, tokens_ref)

    @pl.when(inner == 1)
    def _():
        put(in2_ref, m)
        stack_columns(in3_ref, tokens_ref)

    @pl.when(inner == 0)
    def _():
        put(in3_ref, m)
        stack_columns(in2_ref, tokens_ref)


def pack(where, kv, q, tokens, rows):
    depth = kv.shape[0]
    width = (kv.shape[1] + q.shape[1]) // MEMBERS
    whole = lambda shape: pl.BlockSpec(shape, lambda i, wh: (0, 0))
    piece = jax.ShapeDtypeStruct((depth, width), kv.dtype)
    return pl.pallas_call(
        pack_body,
        grid_spec=pltpu.PrefetchScalarGridSpec(
            num_scalar_prefetch=1,
            grid=(1,),
            in_specs=[
                whole(kv.shape),
                whole(q.shape),
                pl.BlockSpec((rows, tokens.shape[1]), lambda i, wh: (2 * wh[1] + 1, 0)),
            ],
            out_specs=[whole((depth, width))] * 7,
        ),
        out_shape=[piece] * 7,
        compiler_params=params(),
    )(where, kv, q, tokens)


def grouped(seq_size, fsdp_size, tokens, w_query, w_keyval, doc_lengths, norm_gain):
    rows, model = tokens.shape
    depth, head_count, size = w_query.shape
    heads = head_count // MEMBERS
    s = lax.axis_index("seq")
    f = lax.axis_index("fsdp")
    m = lax.rem(s, MEMBERS)
    g = lax.div(s, MEMBERS)
    doc_ends = jnp.cumsum(doc_lengths)

    inner = ((s >> 1) ^ (s >> 2)) & 1 == 1
    where = jnp.stack([m, f, g, inner]).astype(jnp.int32)
    inner_seq = [i for i in range(seq_size) if ((i >> 1) ^ (i >> 2)) & 1 == 1]
    outer_seq = [i for i in range(seq_size) if i not in inner_seq]

    def hop(value, k, only=range(seq_size)):
        return lax.ppermute(value, "seq", [(i, i ^ k) for i in only])

    def side(value, k):
        return lax.ppermute(value, "fsdp", [(i, i ^ k) for i in range(fsdp_size)])

    q_width, kv_width = heads * size, 2 * heads * size
    width = kv_width + q_width
    q_block = kv_width // q_width
    flat_kv = w_keyval.reshape(depth, head_count * 2 * size)
    flat_q = w_query.reshape(depth, head_count * size)

    half = rows // fsdp_size // 2

    history = [[], []]

    def stage(extra, ops, ties="chain"):
        found, before = [], history[-1]
        for chain, move, operand in ops:
            waits = [v for v in extra if not isinstance(v, tuple)]
            waits += [v[1] for v in extra if isinstance(v, tuple) and v[0] == chain]
            if ties == "chain":
                waits += [v for _, v in history[-2]] + [v for c_, v in before if c_ == chain]
            elif ties == "all":
                waits += [v for _, v in before]
            if waits:
                operand = lax.optimization_barrier((operand, tuple(waits)))[0]
            found.append((chain, move(operand)))
        history.append(found)
        return [v for _, v in found]

    def blocks(*ks):
        return jnp.stack([s ^ k for k in ks]).astype(jnp.int32)

    def pairs(inner_hop, outer_hop):
        moves = [(i, i ^ inner_hop) for i in inner_seq if inner_hop]
        moves += [(i, i ^ outer_hop) for i in outer_seq if outer_hop]
        return lambda value: lax.ppermute(value, "seq", moves)

    def pick(a, b):
        return jnp.where(inner, a, b)

    def spread(j, first, second):
        found = []
        for offset, pieces in ((0, first), (half, second)):
            found += [(p, (j, [(e, offset)])) for e, p in zip((0, 2, 1, 3), pieces)]
        return found

    def x(value):
        return hop(value, 1)

    def y(value):
        return side(value, 2)

    def c(value):
        return side(value, 1)

    both_ways = pairs(2, 2)
    part0 = [(tokens, (0, [(None, 0)]))]
    own1 = stacked(where, tokens, half, depth)
    raw = [
        lax.dynamic_slice(w, (0, (m ^ 2) * heads, 0), (depth, heads, w.shape[2]))
        for w in (w_keyval, w_query)
    ]
    r1_kv, r1_q, tz1, tx1 = stage(
        [],
        [("z", pairs(6, 0), raw[0]), ("z", pairs(6, 0), raw[1]), ("z", both_ways, own1), ("x", x, own1)],
    )
    wa, wb, x_first, x_second, own2, in2, in3 = pack(where, flat_kv, flat_q, tokens, half)
    r1 = jnp.concatenate([r1_kv.reshape(depth, -1), r1_q.reshape(depth, -1)], axis=1)
    r2, tx2, yx1, cx1, cz1 = stage(
        [doc_ends],
        [("z", pairs(4, 2), in2), ("x", x, own2), ("y", y, tx1), ("c", c, tx1), ("c", c, tz1)],
    )
    r3, rx1, yx2, cx2, dx1 = stage(
        [], [("z", pairs(2, 4), in3), ("x", x, x_first), ("y", y, tx2), ("c", c, tx2), ("c", c, yx1)]
    )
    r4, tzx1, yz1, dx2 = stage(
        [], [("z", pairs(0, 6), wb), ("x", x, tz1), ("y", y, tz1), ("c", c, yx2)]
    )
    tz2, w4 = pick(r2, r3), pick(r3, r2)
    rx1_kv, rx1_q = rx1[:, :kv_width], rx1[:, kv_width:]
    part1 = spread(1, (tx1, yx1, cx1, dx1), (tx2, yx2, cx2, dx2))
    r5, z5, rx2, yzx1, dz1 = stage(
        [tz2, w4, rx1_kv, rx1_q],
        [("z", pairs(6, 0), rx1), ("z", both_ways, wb), ("x", x, x_second), ("y", y, tzx1), ("c", c, yz1)],
    )
    w6 = pick(r1, r4)
    near = part0 + part1
    n = len(near)
    acc_a = project(
        where, blocks(0, 4, 6), near, [(w, 0, n) for w in (wa, w4, w6)], depth, 0, width
    )
    r6, tzx2, yz2, czx1, dzx1 = stage(
        [acc_a],
        [("z", pairs(4, 2), rx2), ("x", x, tz2), ("y", y, tz2), ("c", c, tzx1), ("c", c, yzx1)],
    )
    rx2_kv, rx2_q = rx2[:, :kv_width], rx2[:, kv_width:]
    r5_q = r5[:, kv_width:]
    rxa = pick(rx2, rx1)
    five, w_five = [0, 4, 6, 1, 2], [wa, w4, w6, rxa, z5]
    first2 = spread(2, (tz1, yz1, cz1, dz1), [None] * 4)[:4]
    acc_a = project(
        where, blocks(*five), near + first2,
        [(w, n, n + 4) for w in w_five[:3]] + [(w, 0, n + 4) for w in w_five[3:]], depth, 0, width,
        starts=[(acc_a, 0, 2 * rows, 0)],
    )
    r7, yzx2, cz2, czx2, dz2 = stage(
        [acc_a, rx2_kv, rx2_q, r5_q],
        [("z", pairs(2, 4), rx1_kv), ("y", y, tzx2), ("c", c, tz2), ("c", c, tzx2), ("c", c, yz2)],
        "all",
    )
    six = blocks(*five, pick(3, 5))
    first3 = spread(3, (tzx1, yzx1, czx1, dzx1), [None] * 4)[:4]
    most = near + first2 + first3
    acc_b = project(
        where, six, most, [(w, n + 4, n + 8) for w in w_five] + [(r6, 0, n + 8)], depth, 0, width,
        starts=[(acc_a, 0, 2 * rows + rows // 2, 0)],
    )
    dzx2, r8 = stage([acc_b], [("c", c, yzx2), ("z", pairs(0, 6), rx2_kv)], "all")
    rest = spread(2, [None] * 4, (tz2, yz2, cz2, dz2))[4:]
    rest += spread(3, [None] * 4, (tzx2, yzx2, czx2, dzx2))[4:]
    acc_c = project(where, six, rest, [(w, 0, 8) for w in w_five + [r6]], depth, 0, width)
    r7q, r8q = stage(
        [acc_c], [("z", pairs(2, 4), rx1_q), ("z", pairs(0, 6), rx2_q)], ties=None
    )

    r8 = lax.optimization_barrier((r8, acc_c))[0]
    every = most + rest
    last = blocks(pick(5, 3), 7)

    def finals(column):
        return [(acc_b, 0, 3 * rows, column), (acc_c, 0, rows, column)]

    keyval, tail, state = project(
        where, last, every, [(w, 0, len(every)) for w in (r7, (r8, r5))],
        depth, 0, kv_width, starts=finals(0), kind=(heads, size), ends=doc_ends,
    )
    other = hop(state, MEMBERS)
    queries = project(
        where, last, every, [(w, 0, len(every)) for w in (r7q, (r8q, r5_q))],
        depth, 0, q_width, starts=finals(q_block), kind="query",
    )

    outs, squares, sent = {}, 0.0, []
    for k in (3, 2, 1, 0):
        if k == 0:
            queries = lax.optimization_barrier((queries, sent[0]))[0]
        outs[k], square = attend(where, doc_ends, k, queries, keyval, tail, other)
        if k:
            outs[k], square = hop(outs[k], k), hop(square, k)
            sent.append(outs[k])
        squares = squares + square
    squares = squares + sum(side(squares, k) for k in range(1, fsdp_size))
    return finish(
        where, [outs[k] for k in range(MEMBERS)], squares, norm_gain[None, :],
        head_count * fsdp_size * size,
    )


def plain(tokens, w_query, w_keyval, doc_lengths, norm_gain):
    rows_here = tokens.shape[0]
    head_count = w_query.shape[1]
    head_size = w_query.shape[2]
    shard_index = lax.axis_index("seq")
    doc_ends = jnp.cumsum(doc_lengths)
    offsets = lax.iota(jnp.int32, rows_here)
    doc_ids = doc_index(shard_index * rows_here + offsets, doc_ends)
    first_doc = doc_ids[0]
    tail_doc = doc_ids[rows_here - 1]

    def project(panel_rows):
        panel = panel_rows.reshape(panel_rows.shape[0], panel_rows.shape[1] * panel_rows.shape[2])
        return jnp.dot(tokens, panel, preferred_element_type=jnp.float32)

    query_sum = project(lax.all_gather(w_query, "seq", axis=0, tiled=True))
    keyval_sum = project(lax.all_gather(w_keyval, "seq", axis=0, tiled=True))
    keyval = (
        jax.nn.silu(keyval_sum).astype(jnp.bfloat16).reshape(rows_here, head_count, 2 * head_size)
    )
    key_rows = keyval[:, :, :head_size]
    values = keyval[:, :, head_size:]
    tail_mask = (doc_ids == tail_doc).astype(jnp.bfloat16)
    tail_state = jnp.einsum(
        "thd,the->hde",
        key_rows * tail_mask[:, None, None],
        values,
        preferred_element_type=jnp.float32,
    )
    states = lax.all_gather(tail_state[None], "seq", axis=0, tiled=True)
    shard_ids = lax.iota(jnp.int32, states.shape[0])
    owner_docs = doc_index(shard_ids * rows_here + rows_here - 1, doc_ends)
    selected = ((shard_ids < shard_index) & (owner_docs == first_doc)).astype(jnp.float32)
    incoming = jnp.sum(selected[:, None, None, None] * states, axis=0)
    queries = jax.nn.silu(query_sum).astype(jnp.bfloat16).reshape(rows_here, head_count, head_size)
    scores = jnp.einsum("thd,shd->hts", queries, key_rows, preferred_element_type=jnp.float32)
    causal = (
        (offsets[:, None] >= offsets[None, :]) & (doc_ids[:, None] == doc_ids[None, :])
    ).astype(jnp.float32)
    weights = (scores * causal[None]).astype(jnp.bfloat16)
    within = jnp.einsum("hts,she->the", weights, values, preferred_element_type=jnp.float32)
    carried = jnp.einsum(
        "thd,hde->the", queries, incoming.astype(jnp.bfloat16), preferred_element_type=jnp.float32
    )
    carried = carried * (doc_ids == first_doc).astype(jnp.float32)[:, None, None]
    mixed = within + carried
    sum_squares = lax.psum(jnp.sum(mixed * mixed, axis=(1, 2)), "fsdp")
    inverse_rms = lax.rsqrt(sum_squares / (head_count * lax.axis_size("fsdp") * head_size) + 1e-06)
    flat = mixed.reshape(rows_here, head_count * head_size)
    return (flat * inverse_rms[:, None] * norm_gain.astype(jnp.float32)[None, :]).astype(
        jnp.bfloat16
    )


def solution(mesh):
    seq_size, fsdp_size = mesh.shape["seq"], mesh.shape["fsdp"]
    if seq_size == 2 * MEMBERS:
        body = functools.partial(grouped, seq_size, fsdp_size)
    else:
        body = plain
    return jax.shard_map(
        body,
        mesh=mesh,
        in_specs=(P("seq", None), P("seq", "fsdp", None), P("seq", "fsdp", None), P(), P("fsdp")),
        out_specs=P("seq", "fsdp"),
        check_vma=False,
    )
```

```python
import functools

import jax
import jax.numpy as jnp
from jax import lax
from jax.experimental import pallas as pl
from jax.experimental.pallas import tpu as pltpu
from jax.sharding import PartitionSpec as P

MEMBERS = 4
VMEM = 60 * 1024 * 1024
VMEM_SMALL = 16 * 1024 * 1024


def doc_index(positions, doc_ends):
    return jnp.sum((positions[:, None] >= doc_ends[None, :]).astype(jnp.int32), axis=1)


def silu(v):
    return v / (1.0 + jnp.exp(-v))


def params(limit=VMEM):
    return pltpu.CompilerParams(vmem_limit_bytes=limit)


def accumulate(step, ranges, t_refs, w_refs, total, start_refs, inner=None):
    edges, at = [], 0
    for ref in t_refs:
        edges.append((at, at + ref.shape[0]))
        at += ref.shape[0]

    @pl.when(step == 0)
    def _():
        at = 0
        for ref in start_refs:
            total[at : at + ref.shape[0], :] = ref[...]
            at += ref.shape[0]
        if at < total.shape[0]:
            total[at:, :] = jnp.zeros((total.shape[0] - at, total.shape[1]), jnp.float32)

    def run(w_ref, low, high):
        chosen = [r[...] for r, (a, b) in zip(t_refs, edges) if low <= a and b <= high]
        lhs = jnp.concatenate(chosen, axis=0) if len(chosen) > 1 else chosen[0]
        total[low:high, :] += jnp.dot(lhs, w_ref[...], preferred_element_type=jnp.float32)

    for w_ref, (first, end, low, high, place) in zip(w_refs, ranges):
        here = (step >= first) & (step < end)
        if place is not None:
            here = here & (inner == place)
        pl.when(here)(functools.partial(run, w_ref, low, high))


def project_body(ranges, starts, *refs):
    k_ref, refs = refs[0], refs[1:]
    arrays = len(ranges)
    parts = len(refs) - arrays - starts - 1
    t_refs, w_refs, refs = refs[:parts], refs[parts : parts + arrays], refs[parts + arrays :]
    accumulate(pl.program_id(0), ranges, t_refs, w_refs, refs[-1], refs[:starts])


def fetch(step, starts, start_refs, held, sems, body):
    width = held.shape[1]
    copies, at = [], 0
    for i, (ref, (block, count, column)) in enumerate(zip(start_refs, starts)):
        part = ref.at[pl.ds(block * count, count), pl.ds(column * width, width)]
        copies.append(pltpu.make_async_copy(part, held.at[pl.ds(at, count), :], sems.at[i]))
        at += count

    @pl.when(step == 0)
    def _():
        for copy in copies:
            copy.start()

    body()

    @pl.when(step == pl.num_programs(0) - 1)
    def _():
        for copy in copies:
            copy.wait()


def settle(places, fsdp_size, where_ref, t_refs, total, held, out_ref):
    m, f = where_ref[0], where_ref[1]
    block_rows = out_ref.shape[0] // MEMBERS
    at = 0
    for ref, (j, spots) in zip(t_refs, places):
        rows = ref.shape[0] // len(spots)
        for e, offset in spots:
            to = (m ^ j) * block_rows
            if e is not None:
                to = to + (f ^ e) * (block_rows // fsdp_size) + offset
            to = pl.multiple_of(to, 16)
            value = silu(total[at : at + rows, :] + held[at : at + rows, :])
            out_ref[pl.ds(to, rows), :] = value.astype(out_ref.dtype)
            at += rows


def activate_body(places, fsdp_size, ranges, starts, where_ref, k_ref, *refs):
    parts, arrays = len(places), len(ranges)
    t_refs, w_refs, refs = refs[:parts], refs[parts : parts + arrays], refs[parts + arrays :]
    start_refs, (out_ref, total, held, sems) = refs[: len(starts)], refs[len(starts) :]
    step = pl.program_id(0)
    run = functools.partial(accumulate, step, ranges, t_refs, w_refs, total, (), where_ref[3])
    fetch(step, starts, start_refs, held, sems, run)

    @pl.when(step == ranges[-1][1] - 1)
    def _():
        settle(places, fsdp_size, where_ref, t_refs, total, held, out_ref)


def keyval_body(places, fsdp_size, ranges, starts, heads, where_ref, k_ref, ends_ref, *refs):
    parts, arrays = len(places), len(ranges)
    t_refs, w_refs, refs = refs[:parts], refs[parts : parts + arrays], refs[parts + arrays :]
    start_refs, refs = refs[: len(starts)], refs[len(starts) :]
    out_ref, tails_ref, state_ref, total, held, sems = refs
    step = pl.program_id(0)
    run = functools.partial(accumulate, step, ranges, t_refs, w_refs, total, (), where_ref[3])
    fetch(step, starts, start_refs, held, sems, run)

    @pl.when(step == ranges[-1][1] - 1)
    def _():
        settle(places, fsdp_size, where_ref, t_refs, total, held, out_ref)
        rows = out_ref.shape[0] // MEMBERS
        size = out_ref.shape[1] // heads // 2
        for b in range(MEMBERS):
            start = (where_ref[2] * MEMBERS + b) * rows
            last = doc_of_scalar(start + rows - 1, ends_ref)
            before = doc_of_scalar(start - 1, ends_ref)
            docs = doc_of(start + lax.broadcasted_iota(jnp.int32, (rows, 1), 0), ends_ref)
            mask = docs == last
            kept = jnp.where(before == last, 1.0, 0.0)
            for h in range(heads):
                at = 2 * h * size
                keys = out_ref[b * rows : (b + 1) * rows, at : at + size]
                keys = jnp.where(mask, keys.astype(jnp.float32), 0.0).astype(keys.dtype)
                values = out_ref[b * rows : (b + 1) * rows, at + size : at + 2 * size]
                tail = lax.dot_general(
                    keys, values, (((0,), (0,)), ((), ())), preferred_element_type=jnp.float32
                )
                tails_ref[b, h] = tail
                state_ref[h] = tail + kept * state_ref[h] if b else tail


def part_rows(part, depth):
    return part.shape[-2] * part.shape[-1] // (depth * lax.axis_size("seq"))


def part_spec(part, depth, block):
    if part.shape[1] == depth:
        return pl.BlockSpec((part_rows(part, depth), depth), lambda *a: (block(*a), 0))
    return pl.BlockSpec((part.shape[0], depth), lambda *a: (0, block(*a)))


def project(where, k_blocks, parts, weights, depth, column, width, starts=(), kind="sum", ends=None):
    counts = [part_rows(p, depth) for p, _ in parts]
    rows = sum(counts)
    ranges, spans, steps = [], [None] * len(parts), 0
    arrays = []
    for w, a, b in weights:
        choices = w if isinstance(w, tuple) else (w,)
        end = steps + choices[0].shape[0] // depth
        for place, choice in enumerate(choices):
            place = place if len(choices) > 1 else None
            ranges.append((steps, end, sum(counts[:a]), sum(counts[:b]), place))
            arrays.append(choice)
        for i in range(a, b):
            spans[i] = (spans[i][0] if spans[i] else steps, end)
        steps = end
    in_specs = [
        part_spec(p, depth, lambda k, kb, *_, s=s: kb[jnp.clip(k, s[0], s[1] - 1)])
        for (p, _), s in zip(parts, spans)
    ]
    in_specs += [
        pl.BlockSpec(
            (depth, width),
            lambda k, *_, r=r, c=column if w.shape[1] > width else 0: (
                jnp.clip(k - r[0], 0, r[1] - r[0] - 1),
                c,
            ),
        )
        for w, r in zip(arrays, ranges)
    ]
    if kind == "sum":
        in_specs += [
            pl.BlockSpec((count, width), lambda k, *_, at=at, c=c: (at, c))
            for _, at, count, c in starts
        ]
    else:
        in_specs += [pl.BlockSpec(memory_space=pl.ANY) for _ in starts]
    operands = [p for p, _ in parts] + arrays + [a for a, _, _, _ in starts]
    whole = pl.BlockSpec((rows, width), lambda k, *_: (0, 0))
    scratch = [
        pltpu.VMEM((rows, width), jnp.float32),
        pltpu.VMEM((rows, width), jnp.float32),
        pltpu.SemaphoreType.DMA((max(len(starts), 1),)),
    ]
    spots = [(at, count, c) for _, at, count, c in starts]
    places, fsdp_size = [p for _, p in parts], lax.axis_size("fsdp")
    if kind == "sum":
        prefetch, scratch = [k_blocks], []
        body = functools.partial(project_body, ranges, len(starts))
        out_specs, out_shape = whole, jax.ShapeDtypeStruct((rows, width), jnp.float32)
    elif kind == "query":
        prefetch = [where, k_blocks]
        body = functools.partial(activate_body, places, fsdp_size, ranges, spots)
        out_specs, out_shape = whole, jax.ShapeDtypeStruct((rows, width), jnp.bfloat16)
    else:
        heads, size = kind
        prefetch = [where, k_blocks, ends]
        body = functools.partial(keyval_body, places, fsdp_size, ranges, spots, heads)
        out_specs = [
            whole,
            pl.BlockSpec((MEMBERS, heads, size, size), lambda k, *_: (0, 0, 0, 0)),
            pl.BlockSpec((heads, size, size), lambda k, *_: (0, 0, 0)),
        ]
        out_shape = [
            jax.ShapeDtypeStruct((rows, width), jnp.bfloat16),
            jax.ShapeDtypeStruct((MEMBERS, heads, size, size), jnp.float32),
            jax.ShapeDtypeStruct((heads, size, size), jnp.float32),
        ]
    at = prefetch.index(k_blocks) if kind == "sum" else 1
    if at:
        for i, p in enumerate(parts):
            s = spans[i]
            in_specs[i] = part_spec(
                p[0], depth, lambda k, wh, kb, *_, s=s: kb[jnp.clip(k, s[0], s[1] - 1)]
            )
    work = sum((r[1] - r[0]) * (r[3] - r[2]) for r in ranges)
    return pl.pallas_call(
        body,
        grid_spec=pltpu.PrefetchScalarGridSpec(
            num_scalar_prefetch=len(prefetch),
            grid=(steps,),
            in_specs=in_specs,
            out_specs=out_specs,
            scratch_shapes=scratch,
        ),
        out_shape=out_shape,
        compiler_params=params(),
        cost_estimate=pl.CostEstimate(
            flops=2 * work * depth * width,
            bytes_accessed=2 * depth * (work + steps * width) + 8 * rows * width,
            transcendentals=0,
        ),
    )(*prefetch, *operands)


def doc_of(positions, ends_ref):
    total = jnp.zeros(positions.shape, jnp.int32)
    for i in range(ends_ref.shape[0]):
        total += (positions >= ends_ref[i]).astype(jnp.int32)
    return total


def doc_of_scalar(position, ends_ref):
    total = jnp.int32(0)
    for i in range(ends_ref.shape[0]):
        total += (position >= ends_ref[i]).astype(jnp.int32)
    return total


def attend_body(place, cut, where_ref, ends_ref, q_ref, kv_ref, tails_ref, other_ref, out_ref, square_ref):
    rows, width = q_ref.shape
    heads, size = other_ref.shape[0], other_ref.shape[1]
    m, g = where_ref[0], where_ref[2]
    block = m ^ place
    origin = g * MEMBERS * rows
    start = origin + block * rows
    before = doc_of_scalar(start - 1, ends_ref)

    edge = doc_of_scalar(origin - 1, ends_ref)
    owner = doc_of_scalar(((g ^ 1) + 1) * MEMBERS * rows - 1, ends_ref)
    state = jnp.where((g == 1) & (owner == edge), 1.0, 0.0) * other_ref[...]
    for i in range(MEMBERS - 1):
        prior = doc_of_scalar(origin + i * rows - 1, ends_ref)
        ended = doc_of_scalar(origin + (i + 1) * rows - 1, ends_ref)
        follows = tails_ref[i] + jnp.where(prior == ended, 1.0, 0.0) * state
        state = jnp.where(i < block, follows, state)
    incoming = state.astype(jnp.bfloat16)

    row_docs = doc_of(start + lax.broadcasted_iota(jnp.int32, (1, rows), 1), ends_ref)
    for begin in range(0, rows, cut):
        seen = begin + cut
        docs = doc_of(start + begin + lax.broadcasted_iota(jnp.int32, (cut, 1), 0), ends_ref)
        at = begin + lax.broadcasted_iota(jnp.int32, (cut, seen), 0)
        behind = lax.broadcasted_iota(jnp.int32, (cut, seen), 1)
        mask = (at >= behind) & (docs == row_docs[:, :seen])
        mixed = []
        for h in range(heads):
            k_at, v_at = 2 * h * size, (2 * h + 1) * size
            q = q_ref[begin:seen, h * size : (h + 1) * size]
            scores = lax.dot_general(
                q, kv_ref[:seen, k_at : k_at + size], (((1,), (1,)), ((), ())),
                preferred_element_type=jnp.float32,
            )
            weights = jnp.where(mask, scores, 0.0).astype(jnp.bfloat16)
            within = jnp.dot(
                weights, kv_ref[:seen, v_at : v_at + size], preferred_element_type=jnp.float32
            )
            carried = jnp.dot(q, incoming[h], preferred_element_type=jnp.float32)
            mixed.append(within + jnp.where(docs == before, carried, 0.0))
        mixed = jnp.concatenate(mixed, axis=1)
        out_ref[begin:seen, :] = mixed.astype(out_ref.dtype)
        sums = lax.dot_general(
            jnp.ones((8, width), jnp.float32), mixed * mixed, (((1,), (1,)), ((), ())),
            preferred_element_type=jnp.float32,
        )
        square_ref[:, begin:seen] = sums[:1]


def attend(where, ends, place, q, kv, tail, other):
    rows, width = q.shape[0] // MEMBERS, q.shape[1]
    heads, size = other.shape[0], other.shape[1]
    cut = rows // 3 if rows % 384 == 0 else rows
    return pl.pallas_call(
        functools.partial(attend_body, place, cut),
        grid_spec=pltpu.PrefetchScalarGridSpec(
            num_scalar_prefetch=2,
            grid=(1,),
            in_specs=[
                pl.BlockSpec((rows, width), lambda i, wh, en: (wh[0] ^ place, 0)),
                pl.BlockSpec((rows, kv.shape[1]), lambda i, wh, en: (wh[0] ^ place, 0)),
                pl.BlockSpec(tail.shape, lambda i, wh, en: (0, 0, 0, 0)),
                pl.BlockSpec(other.shape, lambda i, wh, en: (0, 0, 0)),
            ],
            out_specs=[
                pl.BlockSpec((rows, width), lambda i, wh, en: (0, 0)),
                pl.BlockSpec((1, rows), lambda i, wh, en: (0, 0)),
            ],
        ),
        out_shape=[
            jax.ShapeDtypeStruct((rows, width), jnp.bfloat16),
            jax.ShapeDtypeStruct((1, rows), jnp.float32),
        ],
        compiler_params=params(VMEM_SMALL),
        cost_estimate=pl.CostEstimate(
            flops=3 * rows * rows * width + 2 * rows * width * size,
            bytes_accessed=8 * rows * width,
            transcendentals=0,
        ),
    )(where, ends, q, kv, tail, other)


def finish_body(count, where_ref, *refs):
    squares_ref, gain_ref, out_ref = refs[MEMBERS:]
    rows, width = refs[0].shape
    inverse = lax.rsqrt(squares_ref[...] / count + 1e-06)
    inverse = jnp.transpose(jnp.broadcast_to(inverse, (128, rows)))[:, :1]
    for k in range(MEMBERS):
        at = pl.multiple_of((where_ref[0] ^ k) * width, width)
        gain = gain_ref[:, pl.ds(at, width)].astype(jnp.float32)
        value = refs[k][...].astype(jnp.float32) * inverse * gain
        out_ref[:, pl.ds(at, width)] = value.astype(out_ref.dtype)


def finish(where, parts, squares, gain, count):
    rows, width = parts[0].shape
    cut = rows // 3 if rows % 384 == 0 else rows
    return pl.pallas_call(
        functools.partial(finish_body, count),
        grid_spec=pltpu.PrefetchScalarGridSpec(
            num_scalar_prefetch=1,
            grid=(rows // cut,),
            in_specs=[pl.BlockSpec((cut, width), lambda i, wh: (i, 0)) for _ in parts]
            + [
                pl.BlockSpec((1, cut), lambda i, wh: (0, i)),
                pl.BlockSpec((1, MEMBERS * width), lambda i, wh: (0, 0)),
            ],
            out_specs=pl.BlockSpec((cut, MEMBERS * width), lambda i, wh: (i, 0)),
        ),
        out_shape=jax.ShapeDtypeStruct((rows, MEMBERS * width), jnp.bfloat16),
        compiler_params=params(VMEM_SMALL),
    )(where, *parts, squares, gain)


def stack_columns(out_ref, in_ref):
    rows, depth = in_ref.shape[0], out_ref.shape[1]
    for k in range(out_ref.shape[0] // rows):
        out_ref[k * rows : (k + 1) * rows, :] = in_ref[:, k * depth : (k + 1) * depth]


def stacked_body(where_ref, in_ref, out_ref):
    stack_columns(out_ref, in_ref)


def stacked(where, tokens, rows, depth):
    model = tokens.shape[1]
    return pl.pallas_call(
        stacked_body,
        grid_spec=pltpu.PrefetchScalarGridSpec(
            num_scalar_prefetch=1,
            grid=(1,),
            in_specs=[pl.BlockSpec((rows, model), lambda i, wh: (2 * wh[1], 0))],
            out_specs=pl.BlockSpec((model // depth * rows, depth), lambda i, wh: (0, 0)),
        ),
        out_shape=jax.ShapeDtypeStruct((model // depth * rows, depth), tokens.dtype),
        compiler_params=params(),
    )(where, tokens)


def pack_body(where_ref, kv_ref, q_ref, tokens_ref, a_ref, b_ref, x1_ref, x2_ref, own_ref, in2_ref, in3_ref):
    m, inner = where_ref[0], where_ref[3]
    width = a_ref.shape[1]
    q_width = q_ref.shape[1] // MEMBERS
    kv_width = width - q_width

    def put(ref, member):
        at = pl.multiple_of(member * kv_width, 128)
        ref[:, :kv_width] = kv_ref[:, pl.ds(at, kv_width)]
        at = pl.multiple_of(member * q_width, 128)
        ref[:, kv_width:] = q_ref[:, pl.ds(at, q_width)]

    put(a_ref, m)
    put(b_ref, m ^ 2)
    put(x1_ref, m ^ (1 + 2 * inner))
    put(x2_ref, m ^ (3 - 2 * inner))
    stack_columns(own_ref, tokens_ref)

    @pl.when(inner == 1)
    def _():
        put(in2_ref, m)
        stack_columns(in3_ref, tokens_ref)

    @pl.when(inner == 0)
    def _():
        put(in3_ref, m)
        stack_columns(in2_ref, tokens_ref)


def pack(where, kv, q, tokens, rows):
    depth = kv.shape[0]
    width = (kv.shape[1] + q.shape[1]) // MEMBERS
    whole = lambda shape: pl.BlockSpec(shape, lambda i, wh: (0, 0))
    piece = jax.ShapeDtypeStruct((depth, width), kv.dtype)
    return pl.pallas_call(
        pack_body,
        grid_spec=pltpu.PrefetchScalarGridSpec(
            num_scalar_prefetch=1,
            grid=(1,),
            in_specs=[
                whole(kv.shape),
                whole(q.shape),
                pl.BlockSpec((rows, tokens.shape[1]), lambda i, wh: (2 * wh[1] + 1, 0)),
            ],
            out_specs=[whole((depth, width))] * 7,
        ),
        out_shape=[piece] * 7,
        compiler_params=params(),
    )(where, kv, q, tokens)


def grouped(seq_size, fsdp_size, tokens, w_query, w_keyval, doc_lengths, norm_gain):
    rows, model = tokens.shape
    depth, head_count, size = w_query.shape
    heads = head_count // MEMBERS
    s = lax.axis_index("seq")
    f = lax.axis_index("fsdp")
    m = lax.rem(s, MEMBERS)
    g = lax.div(s, MEMBERS)
    doc_ends = jnp.cumsum(doc_lengths)

    inner = ((s >> 1) ^ (s >> 2)) & 1 == 1
    where = jnp.stack([m, f, g, inner]).astype(jnp.int32)
    inner_seq = [i for i in range(seq_size) if ((i >> 1) ^ (i >> 2)) & 1 == 1]
    outer_seq = [i for i in range(seq_size) if i not in inner_seq]

    def hop(value, k, only=range(seq_size)):
        return lax.ppermute(value, "seq", [(i, i ^ k) for i in only])

    def side(value, k):
        return lax.ppermute(value, "fsdp", [(i, i ^ k) for i in range(fsdp_size)])

    q_width, kv_width = heads * size, 2 * heads * size
    width = kv_width + q_width
    q_block = kv_width // q_width
    flat_kv = w_keyval.reshape(depth, head_count * 2 * size)
    flat_q = w_query.reshape(depth, head_count * size)

    half = rows // fsdp_size // 2

    history = [[], []]

    def stage(extra, ops, ties="chain"):
        found, before = [], history[-1]
        for chain, move, operand in ops:
            waits = [v for v in extra if not isinstance(v, tuple)]
            waits += [v[1] for v in extra if isinstance(v, tuple) and v[0] == chain]
            if ties == "chain":
                waits += [v for _, v in history[-2]] + [v for c_, v in before if c_ == chain]
            elif ties == "all":
                waits += [v for _, v in before]
            if waits:
                operand = lax.optimization_barrier((operand, tuple(waits)))[0]
            found.append((chain, move(operand)))
        history.append(found)
        return [v for _, v in found]

    def blocks(*ks):
        return jnp.stack([s ^ k for k in ks]).astype(jnp.int32)

    def pairs(inner_hop, outer_hop):
        moves = [(i, i ^ inner_hop) for i in inner_seq if inner_hop]
        moves += [(i, i ^ outer_hop) for i in outer_seq if outer_hop]
        return lambda value: lax.ppermute(value, "seq", moves)

    def pick(a, b):
        return jnp.where(inner, a, b)

    def spread(j, first, second):
        found = []
        for offset, pieces in ((0, first), (half, second)):
            found += [(p, (j, [(e, offset)])) for e, p in zip((0, 2, 1, 3), pieces)]
        return found

    def x(value):
        return hop(value, 1)

    def y(value):
        return side(value, 2)

    def c(value):
        return side(value, 1)

    both_ways = pairs(2, 2)
    part0 = [(tokens, (0, [(None, 0)]))]
    own1 = stacked(where, tokens, half, depth)
    raw = [
        lax.dynamic_slice(w, (0, (m ^ 2) * heads, 0), (depth, heads, w.shape[2]))
        for w in (w_keyval, w_query)
    ]
    r1_kv, r1_q, tz1, tx1 = stage(
        [],
        [("z", pairs(6, 0), raw[0]), ("z", pairs(6, 0), raw[1]), ("z", both_ways, own1), ("x", x, own1)],
    )
    wa, wb, x_first, x_second, own2, in2, in3 = pack(where, flat_kv, flat_q, tokens, half)
    r1 = jnp.concatenate([r1_kv.reshape(depth, -1), r1_q.reshape(depth, -1)], axis=1)
    r2, tx2, yx1, cx1, cz1 = stage(
        [doc_ends],
        [("z", pairs(4, 2), in2), ("x", x, own2), ("y", y, tx1), ("c", c, tx1), ("c", c, tz1)],
    )
    r3, rx1, yx2, cx2, dx1 = stage(
        [], [("z", pairs(2, 4), in3), ("x", x, x_first), ("y", y, tx2), ("c", c, tx2), ("c", c, yx1)]
    )
    r4, tzx1, yz1, dx2 = stage(
        [], [("z", pairs(0, 6), wb), ("x", x, tz1), ("y", y, tz1), ("c", c, yx2)]
    )
    tz2, w4 = pick(r2, r3), pick(r3, r2)
    rx1_kv, rx1_q = rx1[:, :kv_width], rx1[:, kv_width:]
    part1 = spread(1, (tx1, yx1, cx1, dx1), (tx2, yx2, cx2, dx2))
    r5, z5, rx2, yzx1, dz1 = stage(
        [tz2, w4, rx1_kv, rx1_q],
        [("z", pairs(6, 0), rx1), ("z", both_ways, wb), ("x", x, x_second), ("y", y, tzx1), ("c", c, yz1)],
    )
    w6 = pick(r1, r4)
    near = part0 + part1
    n = len(near)
    acc_a = project(
        where, blocks(0, 4, 6), near, [(w, 0, n) for w in (wa, w4, w6)], depth, 0, width
    )
    r6, tzx2, yz2, czx1, dzx1 = stage(
        [acc_a],
        [("z", pairs(4, 2), rx2), ("x", x, tz2), ("y", y, tz2), ("c", c, tzx1), ("c", c, yzx1)],
    )
    rx2_kv, rx2_q = rx2[:, :kv_width], rx2[:, kv_width:]
    r5_q = r5[:, kv_width:]
    rxa = pick(rx2, rx1)
    five, w_five = [0, 4, 6, 1, 2], [wa, w4, w6, rxa, z5]
    six, last = blocks(*five, pick(3, 5)), blocks(pick(5, 3), 7)
    first2 = spread(2, (tz1, yz1, cz1, dz1), [None] * 4)[:4]
    acc_a = project(
        where, blocks(*five), near + first2,
        [(w, n, n + 4) for w in w_five[:3]] + [(w, 0, n + 4) for w in w_five[3:]], depth, 0, width,
        starts=[(acc_a, 0, 2 * rows, 0)],
    )
    r7, yzx2, cz2, czx2, dz2 = stage(
        [acc_a, rx2_kv, rx2_q, r5_q, six, last],
        [("z", pairs(2, 4), rx1_kv), ("y", y, tzx2), ("c", c, tz2), ("c", c, tzx2), ("c", c, yz2)],
        "all",
    )
    first3 = spread(3, (tzx1, yzx1, czx1, dzx1), [None] * 4)[:4]
    most = near + first2 + first3
    acc_b = project(
        where, six, most, [(w, n + 4, n + 8) for w in w_five] + [(r6, 0, n + 8)], depth, 0, width,
        starts=[(acc_a, 0, 2 * rows + rows // 2, 0)],
    )
    dzx2, r8 = stage([acc_b], [("c", c, yzx2), ("z", pairs(0, 6), rx2_kv)], "all")
    rest = spread(2, [None] * 4, (tz2, yz2, cz2, dz2))[4:]
    rest += spread(3, [None] * 4, (tzx2, yzx2, czx2, dzx2))[4:]
    acc_c = project(where, six, rest, [(w, 0, 8) for w in w_five + [r6]], depth, 0, width)
    r7q, r8q = stage(
        [acc_c], [("z", pairs(2, 4), rx1_q), ("z", pairs(0, 6), rx2_q)], ties=None
    )

    r8 = lax.optimization_barrier((r8, acc_c))[0]
    every = most + rest

    def finals(column):
        return [(acc_b, 0, 3 * rows, column), (acc_c, 0, rows, column)]

    keyval, tail, state = project(
        where, last, every, [(w, 0, len(every)) for w in (r7, (r8, r5))],
        depth, 0, kv_width, starts=finals(0), kind=(heads, size), ends=doc_ends,
    )
    other = hop(state, MEMBERS)
    queries = project(
        where, last, every, [(w, 0, len(every)) for w in (r7q, (r8q, r5_q))],
        depth, 0, q_width, starts=finals(q_block), kind="query",
    )

    outs, squares, sent = {}, 0.0, []
    for k in (3, 2, 1, 0):
        if k == 0:
            queries = lax.optimization_barrier((queries, sent[0]))[0]
        outs[k], square = attend(where, doc_ends, k, queries, keyval, tail, other)
        if k:
            outs[k], square = hop(outs[k], k), hop(square, k)
            sent.append(outs[k])
        squares = squares + square
    squares = squares + sum(side(squares, k) for k in range(1, fsdp_size))
    return finish(
        where, [outs[k] for k in range(MEMBERS)], squares, norm_gain[None, :],
        head_count * fsdp_size * size,
    )


def plain(tokens, w_query, w_keyval, doc_lengths, norm_gain):
    rows_here = tokens.shape[0]
    head_count = w_query.shape[1]
    head_size = w_query.shape[2]
    shard_index = lax.axis_index("seq")
    doc_ends = jnp.cumsum(doc_lengths)
    offsets = lax.iota(jnp.int32, rows_here)
    doc_ids = doc_index(shard_index * rows_here + offsets, doc_ends)
    first_doc = doc_ids[0]
    tail_doc = doc_ids[rows_here - 1]

    def project(panel_rows):
        panel = panel_rows.reshape(panel_rows.shape[0], panel_rows.shape[1] * panel_rows.shape[2])
        return jnp.dot(tokens, panel, preferred_element_type=jnp.float32)

    query_sum = project(lax.all_gather(w_query, "seq", axis=0, tiled=True))
    keyval_sum = project(lax.all_gather(w_keyval, "seq", axis=0, tiled=True))
    keyval = (
        jax.nn.silu(keyval_sum).astype(jnp.bfloat16).reshape(rows_here, head_count, 2 * head_size)
    )
    key_rows = keyval[:, :, :head_size]
    values = keyval[:, :, head_size:]
    tail_mask = (doc_ids == tail_doc).astype(jnp.bfloat16)
    tail_state = jnp.einsum(
        "thd,the->hde",
        key_rows * tail_mask[:, None, None],
        values,
        preferred_element_type=jnp.float32,
    )
    states = lax.all_gather(tail_state[None], "seq", axis=0, tiled=True)
    shard_ids = lax.iota(jnp.int32, states.shape[0])
    owner_docs = doc_index(shard_ids * rows_here + rows_here - 1, doc_ends)
    selected = ((shard_ids < shard_index) & (owner_docs == first_doc)).astype(jnp.float32)
    incoming = jnp.sum(selected[:, None, None, None] * states, axis=0)
    queries = jax.nn.silu(query_sum).astype(jnp.bfloat16).reshape(rows_here, head_count, head_size)
    scores = jnp.einsum("thd,shd->hts", queries, key_rows, preferred_element_type=jnp.float32)
    causal = (
        (offsets[:, None] >= offsets[None, :]) & (doc_ids[:, None] == doc_ids[None, :])
    ).astype(jnp.float32)
    weights = (scores * causal[None]).astype(jnp.bfloat16)
    within = jnp.einsum("hts,she->the", weights, values, preferred_element_type=jnp.float32)
    carried = jnp.einsum(
        "thd,hde->the", queries, incoming.astype(jnp.bfloat16), preferred_element_type=jnp.float32
    )
    carried = carried * (doc_ids == first_doc).astype(jnp.float32)[:, None, None]
    mixed = within + carried
    sum_squares = lax.psum(jnp.sum(mixed * mixed, axis=(1, 2)), "fsdp")
    inverse_rms = lax.rsqrt(sum_squares / (head_count * lax.axis_size("fsdp") * head_size) + 1e-06)
    flat = mixed.reshape(rows_here, head_count * head_size)
    return (flat * inverse_rms[:, None] * norm_gain.astype(jnp.float32)[None, :]).astype(
        jnp.bfloat16
    )


def solution(mesh):
    seq_size, fsdp_size = mesh.shape["seq"], mesh.shape["fsdp"]

    def body(tokens, w_query, *rest):
        rows, (depth, head_count, _) = tokens.shape[0], w_query.shape
        fits = seq_size == 2 * MEMBERS and fsdp_size == 4 and head_count % MEMBERS == 0
        if fits and rows == depth and rows % 128 == 0:
            return grouped(seq_size, fsdp_size, tokens, w_query, *rest)
        return plain(tokens, w_query, *rest)

    return jax.shard_map(
        body,
        mesh=mesh,
        in_specs=(P("seq", None), P("seq", "fsdp", None), P("seq", "fsdp", None), P(), P("fsdp")),
        out_specs=P("seq", "fsdp"),
        check_vma=False,
    )
```

```python
import functools

import jax
import jax.numpy as jnp
from jax import lax
from jax.experimental import pallas as pl
from jax.experimental.pallas import tpu as pltpu
from jax.sharding import PartitionSpec as P

MEMBERS = 4
VMEM = 60 * 1024 * 1024
VMEM_SMALL = 16 * 1024 * 1024


def doc_index(positions, doc_ends):
    return jnp.sum((positions[:, None] >= doc_ends[None, :]).astype(jnp.int32), axis=1)


def silu(v):
    return v / (1.0 + jnp.exp(-v))


def params(limit=VMEM):
    return pltpu.CompilerParams(vmem_limit_bytes=limit)


def accumulate(step, ranges, t_refs, w_refs, total, start_refs, inner=None):
    edges, at = [], 0
    for ref in t_refs:
        edges.append((at, at + ref.shape[0]))
        at += ref.shape[0]

    @pl.when(step == 0)
    def _():
        at = 0
        for ref in start_refs:
            total[at : at + ref.shape[0], :] = ref[...]
            at += ref.shape[0]
        if at < total.shape[0]:
            total[at:, :] = jnp.zeros((total.shape[0] - at, total.shape[1]), jnp.float32)

    def run(w_ref, low, high):
        chosen = [r[...] for r, (a, b) in zip(t_refs, edges) if low <= a and b <= high]
        lhs = jnp.concatenate(chosen, axis=0) if len(chosen) > 1 else chosen[0]
        total[low:high, :] += jnp.dot(lhs, w_ref[...], preferred_element_type=jnp.float32)

    for w_ref, (first, end, low, high, place) in zip(w_refs, ranges):
        here = (step >= first) & (step < end)
        if place is not None:
            here = here & (inner == place)
        pl.when(here)(functools.partial(run, w_ref, low, high))


def project_body(ranges, starts, *refs):
    k_ref, refs = refs[0], refs[1:]
    arrays = len(ranges)
    parts = len(refs) - arrays - starts - 1
    t_refs, w_refs, refs = refs[:parts], refs[parts : parts + arrays], refs[parts + arrays :]
    accumulate(pl.program_id(0), ranges, t_refs, w_refs, refs[-1], refs[:starts])


def fetch(step, starts, start_refs, held, sems, body):
    width = held.shape[1]
    copies, at = [], 0
    for i, (ref, (block, count, column)) in enumerate(zip(start_refs, starts)):
        part = ref.at[pl.ds(block * count, count), pl.ds(column * width, width)]
        copies.append(pltpu.make_async_copy(part, held.at[pl.ds(at, count), :], sems.at[i]))
        at += count

    @pl.when(step == 0)
    def _():
        for copy in copies:
            copy.start()

    body()

    @pl.when(step == pl.num_programs(0) - 1)
    def _():
        for copy in copies:
            copy.wait()


def settle(places, fsdp_size, where_ref, t_refs, total, held, out_ref):
    m, f = where_ref[0], where_ref[1]
    block_rows = out_ref.shape[0] // MEMBERS
    at = 0
    for ref, (j, spots) in zip(t_refs, places):
        rows = ref.shape[0] // len(spots)
        for e, offset in spots:
            to = (m ^ j) * block_rows
            if e is not None:
                to = to + (f ^ e) * (block_rows // fsdp_size) + offset
            to = pl.multiple_of(to, 16)
            value = silu(total[at : at + rows, :] + held[at : at + rows, :])
            out_ref[pl.ds(to, rows), :] = value.astype(out_ref.dtype)
            at += rows


def activate_body(places, fsdp_size, ranges, starts, where_ref, k_ref, *refs):
    parts, arrays = len(places), len(ranges)
    t_refs, w_refs, refs = refs[:parts], refs[parts : parts + arrays], refs[parts + arrays :]
    start_refs, (out_ref, total, held, sems) = refs[: len(starts)], refs[len(starts) :]
    step = pl.program_id(0)
    run = functools.partial(accumulate, step, ranges, t_refs, w_refs, total, (), where_ref[3])
    fetch(step, starts, start_refs, held, sems, run)

    @pl.when(step == ranges[-1][1] - 1)
    def _():
        settle(places, fsdp_size, where_ref, t_refs, total, held, out_ref)


def keyval_body(places, fsdp_size, ranges, starts, heads, where_ref, k_ref, ends_ref, *refs):
    parts, arrays = len(places), len(ranges)
    t_refs, w_refs, refs = refs[:parts], refs[parts : parts + arrays], refs[parts + arrays :]
    start_refs, refs = refs[: len(starts)], refs[len(starts) :]
    out_ref, tails_ref, state_ref, total, held, sems = refs
    step = pl.program_id(0)
    run = functools.partial(accumulate, step, ranges, t_refs, w_refs, total, (), where_ref[3])
    fetch(step, starts, start_refs, held, sems, run)

    @pl.when(step == ranges[-1][1] - 1)
    def _():
        settle(places, fsdp_size, where_ref, t_refs, total, held, out_ref)
        rows = out_ref.shape[0] // MEMBERS
        size = out_ref.shape[1] // heads // 2
        for b in range(MEMBERS):
            start = (where_ref[2] * MEMBERS + b) * rows
            last = doc_of_scalar(start + rows - 1, ends_ref)
            before = doc_of_scalar(start - 1, ends_ref)
            docs = doc_of(start + lax.broadcasted_iota(jnp.int32, (rows, 1), 0), ends_ref)
            mask = docs == last
            kept = jnp.where(before == last, 1.0, 0.0)
            for h in range(heads):
                at = 2 * h * size
                keys = out_ref[b * rows : (b + 1) * rows, at : at + size]
                keys = jnp.where(mask, keys.astype(jnp.float32), 0.0).astype(keys.dtype)
                values = out_ref[b * rows : (b + 1) * rows, at + size : at + 2 * size]
                tail = lax.dot_general(
                    keys, values, (((0,), (0,)), ((), ())), preferred_element_type=jnp.float32
                )
                tails_ref[b, h] = tail
                state_ref[h] = tail + kept * state_ref[h] if b else tail


def part_rows(part, depth):
    return part.shape[-2] * part.shape[-1] // (depth * lax.axis_size("seq"))


def part_spec(part, depth, block):
    if part.shape[1] == depth:
        return pl.BlockSpec((part_rows(part, depth), depth), lambda *a: (block(*a), 0))
    return pl.BlockSpec((part.shape[0], depth), lambda *a: (0, block(*a)))


def project(where, k_blocks, parts, weights, depth, column, width, starts=(), kind="sum", ends=None):
    counts = [part_rows(p, depth) for p, _ in parts]
    rows = sum(counts)
    ranges, spans, steps = [], [None] * len(parts), 0
    arrays = []
    for w, a, b in weights:
        choices = w if isinstance(w, tuple) else (w,)
        end = steps + choices[0].shape[0] // depth
        for place, choice in enumerate(choices):
            place = place if len(choices) > 1 else None
            ranges.append((steps, end, sum(counts[:a]), sum(counts[:b]), place))
            arrays.append(choice)
        for i in range(a, b):
            spans[i] = (spans[i][0] if spans[i] else steps, end)
        steps = end
    in_specs = [
        part_spec(p, depth, lambda k, kb, *_, s=s: kb[jnp.clip(k, s[0], s[1] - 1)])
        for (p, _), s in zip(parts, spans)
    ]
    in_specs += [
        pl.BlockSpec(
            (depth, width),
            lambda k, *_, r=r, c=column if w.shape[1] > width else 0: (
                jnp.clip(k - r[0], 0, r[1] - r[0] - 1),
                c,
            ),
        )
        for w, r in zip(arrays, ranges)
    ]
    if kind == "sum":
        in_specs += [
            pl.BlockSpec((count, width), lambda k, *_, at=at, c=c: (at, c))
            for _, at, count, c in starts
        ]
    else:
        in_specs += [pl.BlockSpec(memory_space=pl.ANY) for _ in starts]
    operands = [p for p, _ in parts] + arrays + [a for a, _, _, _ in starts]
    whole = pl.BlockSpec((rows, width), lambda k, *_: (0, 0))
    scratch = [
        pltpu.VMEM((rows, width), jnp.float32),
        pltpu.VMEM((rows, width), jnp.float32),
        pltpu.SemaphoreType.DMA((max(len(starts), 1),)),
    ]
    spots = [(at, count, c) for _, at, count, c in starts]
    places, fsdp_size = [p for _, p in parts], lax.axis_size("fsdp")
    if kind == "sum":
        prefetch, scratch = [k_blocks], []
        body = functools.partial(project_body, ranges, len(starts))
        out_specs, out_shape = whole, jax.ShapeDtypeStruct((rows, width), jnp.float32)
    elif kind == "query":
        prefetch = [where, k_blocks]
        body = functools.partial(activate_body, places, fsdp_size, ranges, spots)
        out_specs, out_shape = whole, jax.ShapeDtypeStruct((rows, width), jnp.bfloat16)
    else:
        heads, size = kind
        prefetch = [where, k_blocks, ends]
        body = functools.partial(keyval_body, places, fsdp_size, ranges, spots, heads)
        out_specs = [
            whole,
            pl.BlockSpec((MEMBERS, heads, size, size), lambda k, *_: (0, 0, 0, 0)),
            pl.BlockSpec((heads, size, size), lambda k, *_: (0, 0, 0)),
        ]
        out_shape = [
            jax.ShapeDtypeStruct((rows, width), jnp.bfloat16),
            jax.ShapeDtypeStruct((MEMBERS, heads, size, size), jnp.float32),
            jax.ShapeDtypeStruct((heads, size, size), jnp.float32),
        ]
    at = prefetch.index(k_blocks) if kind == "sum" else 1
    if at:
        for i, p in enumerate(parts):
            s = spans[i]
            in_specs[i] = part_spec(
                p[0], depth, lambda k, wh, kb, *_, s=s: kb[jnp.clip(k, s[0], s[1] - 1)]
            )
    work = sum((r[1] - r[0]) * (r[3] - r[2]) for r in ranges)
    return pl.pallas_call(
        body,
        grid_spec=pltpu.PrefetchScalarGridSpec(
            num_scalar_prefetch=len(prefetch),
            grid=(steps,),
            in_specs=in_specs,
            out_specs=out_specs,
            scratch_shapes=scratch,
        ),
        out_shape=out_shape,
        compiler_params=params(),
        cost_estimate=pl.CostEstimate(
            flops=2 * work * depth * width,
            bytes_accessed=2 * depth * (work + steps * width) + 8 * rows * width,
            transcendentals=0,
        ),
    )(*prefetch, *operands)


def doc_of(positions, ends_ref):
    total = jnp.zeros(positions.shape, jnp.int32)
    for i in range(ends_ref.shape[0]):
        total += (positions >= ends_ref[i]).astype(jnp.int32)
    return total


def doc_of_scalar(position, ends_ref):
    total = jnp.int32(0)
    for i in range(ends_ref.shape[0]):
        total += (position >= ends_ref[i]).astype(jnp.int32)
    return total


def attend_body(place, cut, where_ref, ends_ref, q_ref, kv_ref, tails_ref, other_ref, out_ref, square_ref):
    rows, width = q_ref.shape
    heads, size = other_ref.shape[0], other_ref.shape[1]
    m, g = where_ref[0], where_ref[2]
    block = m ^ place
    origin = g * MEMBERS * rows
    start = origin + block * rows
    before = doc_of_scalar(start - 1, ends_ref)

    edge = doc_of_scalar(origin - 1, ends_ref)
    owner = doc_of_scalar(((g ^ 1) + 1) * MEMBERS * rows - 1, ends_ref)
    state = jnp.where((g == 1) & (owner == edge), 1.0, 0.0) * other_ref[...]
    for i in range(MEMBERS - 1):
        prior = doc_of_scalar(origin + i * rows - 1, ends_ref)
        ended = doc_of_scalar(origin + (i + 1) * rows - 1, ends_ref)
        follows = tails_ref[i] + jnp.where(prior == ended, 1.0, 0.0) * state
        state = jnp.where(i < block, follows, state)
    incoming = state.astype(jnp.bfloat16)

    row_docs = doc_of(start + lax.broadcasted_iota(jnp.int32, (1, rows), 1), ends_ref)
    for begin in range(0, rows, cut):
        seen = begin + cut
        docs = doc_of(start + begin + lax.broadcasted_iota(jnp.int32, (cut, 1), 0), ends_ref)
        at = begin + lax.broadcasted_iota(jnp.int32, (cut, seen), 0)
        behind = lax.broadcasted_iota(jnp.int32, (cut, seen), 1)
        mask = (at >= behind) & (docs == row_docs[:, :seen])
        mixed = []
        for h in range(heads):
            k_at, v_at = 2 * h * size, (2 * h + 1) * size
            q = q_ref[begin:seen, h * size : (h + 1) * size]
            scores = lax.dot_general(
                q, kv_ref[:seen, k_at : k_at + size], (((1,), (1,)), ((), ())),
                preferred_element_type=jnp.float32,
            )
            weights = jnp.where(mask, scores, 0.0).astype(jnp.bfloat16)
            within = jnp.dot(
                weights, kv_ref[:seen, v_at : v_at + size], preferred_element_type=jnp.float32
            )
            carried = jnp.dot(q, incoming[h], preferred_element_type=jnp.float32)
            mixed.append(within + jnp.where(docs == before, carried, 0.0))
        mixed = jnp.concatenate(mixed, axis=1)
        out_ref[begin:seen, :] = mixed.astype(out_ref.dtype)
        sums = lax.dot_general(
            jnp.ones((8, width), jnp.float32), mixed * mixed, (((1,), (1,)), ((), ())),
            preferred_element_type=jnp.float32,
        )
        square_ref[:, begin:seen] = sums[:1]


def attend(where, ends, place, q, kv, tail, other):
    rows, width = q.shape[0] // MEMBERS, q.shape[1]
    heads, size = other.shape[0], other.shape[1]
    cut = rows // 3 if rows % 384 == 0 else rows
    return pl.pallas_call(
        functools.partial(attend_body, place, cut),
        grid_spec=pltpu.PrefetchScalarGridSpec(
            num_scalar_prefetch=2,
            grid=(1,),
            in_specs=[
                pl.BlockSpec((rows, width), lambda i, wh, en: (wh[0] ^ place, 0)),
                pl.BlockSpec((rows, kv.shape[1]), lambda i, wh, en: (wh[0] ^ place, 0)),
                pl.BlockSpec(tail.shape, lambda i, wh, en: (0, 0, 0, 0)),
                pl.BlockSpec(other.shape, lambda i, wh, en: (0, 0, 0)),
            ],
            out_specs=[
                pl.BlockSpec((rows, width), lambda i, wh, en: (0, 0)),
                pl.BlockSpec((1, rows), lambda i, wh, en: (0, 0)),
            ],
        ),
        out_shape=[
            jax.ShapeDtypeStruct((rows, width), jnp.bfloat16),
            jax.ShapeDtypeStruct((1, rows), jnp.float32),
        ],
        compiler_params=params(VMEM_SMALL),
        cost_estimate=pl.CostEstimate(
            flops=3 * rows * rows * width + 2 * rows * width * size,
            bytes_accessed=8 * rows * width,
            transcendentals=0,
        ),
    )(where, ends, q, kv, tail, other)


def finish_body(count, where_ref, *refs):
    squares_ref, gain_ref, out_ref = refs[MEMBERS:]
    rows, width = refs[0].shape
    inverse = lax.rsqrt(squares_ref[...] / count + 1e-06)
    inverse = jnp.transpose(jnp.broadcast_to(inverse, (128, rows)))[:, :1]
    for k in range(MEMBERS):
        at = pl.multiple_of((where_ref[0] ^ k) * width, width)
        gain = gain_ref[:, pl.ds(at, width)].astype(jnp.float32)
        value = refs[k][...].astype(jnp.float32) * inverse * gain
        out_ref[:, pl.ds(at, width)] = value.astype(out_ref.dtype)


def finish(where, parts, squares, gain, count):
    rows, width = parts[0].shape
    cut = rows // 2 if rows % 256 == 0 else rows
    return pl.pallas_call(
        functools.partial(finish_body, count),
        grid_spec=pltpu.PrefetchScalarGridSpec(
            num_scalar_prefetch=1,
            grid=(rows // cut,),
            in_specs=[pl.BlockSpec((cut, width), lambda i, wh: (i, 0)) for _ in parts]
            + [
                pl.BlockSpec((1, cut), lambda i, wh: (0, i)),
                pl.BlockSpec((1, MEMBERS * width), lambda i, wh: (0, 0)),
            ],
            out_specs=pl.BlockSpec((cut, MEMBERS * width), lambda i, wh: (i, 0)),
        ),
        out_shape=jax.ShapeDtypeStruct((rows, MEMBERS * width), jnp.bfloat16),
        compiler_params=params(VMEM_SMALL),
    )(where, *parts, squares, gain)


def stack_columns(out_ref, in_ref):
    rows, depth = in_ref.shape[0], out_ref.shape[1]
    for k in range(out_ref.shape[0] // rows):
        out_ref[k * rows : (k + 1) * rows, :] = in_ref[:, k * depth : (k + 1) * depth]


def stacked_body(where_ref, in_ref, out_ref):
    stack_columns(out_ref, in_ref)


def stacked(where, tokens, rows, depth):
    model = tokens.shape[1]
    return pl.pallas_call(
        stacked_body,
        grid_spec=pltpu.PrefetchScalarGridSpec(
            num_scalar_prefetch=1,
            grid=(1,),
            in_specs=[pl.BlockSpec((rows, model), lambda i, wh: (2 * wh[1], 0))],
            out_specs=pl.BlockSpec((model // depth * rows, depth), lambda i, wh: (0, 0)),
        ),
        out_shape=jax.ShapeDtypeStruct((model // depth * rows, depth), tokens.dtype),
        compiler_params=params(),
    )(where, tokens)


def pack_body(where_ref, kv_ref, q_ref, tokens_ref, a_ref, b_ref, x1_ref, x2_ref, own_ref, in2_ref, in3_ref):
    m, inner = where_ref[0], where_ref[3]
    width = a_ref.shape[1]
    q_width = q_ref.shape[1] // MEMBERS
    kv_width = width - q_width

    def put(ref, member):
        at = pl.multiple_of(member * kv_width, 128)
        ref[:, :kv_width] = kv_ref[:, pl.ds(at, kv_width)]
        at = pl.multiple_of(member * q_width, 128)
        ref[:, kv_width:] = q_ref[:, pl.ds(at, q_width)]

    put(a_ref, m)
    put(b_ref, m ^ 2)
    put(x1_ref, m ^ (1 + 2 * inner))
    put(x2_ref, m ^ (3 - 2 * inner))
    stack_columns(own_ref, tokens_ref)

    @pl.when(inner == 1)
    def _():
        put(in2_ref, m)
        stack_columns(in3_ref, tokens_ref)

    @pl.when(inner == 0)
    def _():
        put(in3_ref, m)
        stack_columns(in2_ref, tokens_ref)


def pack(where, kv, q, tokens, rows):
    depth = kv.shape[0]
    width = (kv.shape[1] + q.shape[1]) // MEMBERS
    whole = lambda shape: pl.BlockSpec(shape, lambda i, wh: (0, 0))
    piece = jax.ShapeDtypeStruct((depth, width), kv.dtype)
    return pl.pallas_call(
        pack_body,
        grid_spec=pltpu.PrefetchScalarGridSpec(
            num_scalar_prefetch=1,
            grid=(1,),
            in_specs=[
                whole(kv.shape),
                whole(q.shape),
                pl.BlockSpec((rows, tokens.shape[1]), lambda i, wh: (2 * wh[1] + 1, 0)),
            ],
            out_specs=[whole((depth, width))] * 7,
        ),
        out_shape=[piece] * 7,
        compiler_params=params(),
    )(where, kv, q, tokens)


def grouped(seq_size, fsdp_size, tokens, w_query, w_keyval, doc_lengths, norm_gain):
    rows, model = tokens.shape
    depth, head_count, size = w_query.shape
    heads = head_count // MEMBERS
    s = lax.axis_index("seq")
    f = lax.axis_index("fsdp")
    m = lax.rem(s, MEMBERS)
    g = lax.div(s, MEMBERS)
    doc_ends = jnp.cumsum(doc_lengths)

    inner = ((s >> 1) ^ (s >> 2)) & 1 == 1
    where = jnp.stack([m, f, g, inner]).astype(jnp.int32)
    inner_seq = [i for i in range(seq_size) if ((i >> 1) ^ (i >> 2)) & 1 == 1]
    outer_seq = [i for i in range(seq_size) if i not in inner_seq]

    def hop(value, k, only=range(seq_size)):
        return lax.ppermute(value, "seq", [(i, i ^ k) for i in only])

    def side(value, k):
        return lax.ppermute(value, "fsdp", [(i, i ^ k) for i in range(fsdp_size)])

    q_width, kv_width = heads * size, 2 * heads * size
    width = kv_width + q_width
    q_block = kv_width // q_width
    flat_kv = w_keyval.reshape(depth, head_count * 2 * size)
    flat_q = w_query.reshape(depth, head_count * size)

    half = rows // fsdp_size // 2

    history = [[], []]

    def stage(extra, ops, ties="chain"):
        found, before = [], history[-1]
        for chain, move, operand in ops:
            waits = [v for v in extra if not isinstance(v, tuple)]
            waits += [v[1] for v in extra if isinstance(v, tuple) and v[0] == chain]
            if ties == "chain":
                waits += [v for _, v in history[-2]] + [v for c_, v in before if c_ == chain]
            elif ties == "all":
                waits += [v for _, v in before]
            if waits:
                operand = lax.optimization_barrier((operand, tuple(waits)))[0]
            found.append((chain, move(operand)))
        history.append(found)
        return [v for _, v in found]

    def blocks(*ks):
        return jnp.stack([s ^ k for k in ks]).astype(jnp.int32)

    def pairs(inner_hop, outer_hop):
        moves = [(i, i ^ inner_hop) for i in inner_seq if inner_hop]
        moves += [(i, i ^ outer_hop) for i in outer_seq if outer_hop]
        return lambda value: lax.ppermute(value, "seq", moves)

    def pick(a, b):
        return jnp.where(inner, a, b)

    def spread(j, first, second):
        found = []
        for offset, pieces in ((0, first), (half, second)):
            found += [(p, (j, [(e, offset)])) for e, p in zip((0, 2, 1, 3), pieces)]
        return found

    def x(value):
        return hop(value, 1)

    def y(value):
        return side(value, 2)

    def c(value):
        return side(value, 1)

    both_ways = pairs(2, 2)
    part0 = [(tokens, (0, [(None, 0)]))]
    own1 = stacked(where, tokens, half, depth)
    raw = [
        lax.dynamic_slice(w, (0, (m ^ 2) * heads, 0), (depth, heads, w.shape[2]))
        for w in (w_keyval, w_query)
    ]
    r1_kv, r1_q, tz1, tx1 = stage(
        [],
        [("z", pairs(6, 0), raw[0]), ("z", pairs(6, 0), raw[1]), ("z", both_ways, own1), ("x", x, own1)],
    )
    wa, wb, x_first, x_second, own2, in2, in3 = pack(where, flat_kv, flat_q, tokens, half)
    r1 = jnp.concatenate([r1_kv.reshape(depth, -1), r1_q.reshape(depth, -1)], axis=1)
    r2, tx2, yx1, cx1, cz1 = stage(
        [doc_ends],
        [("z", pairs(4, 2), in2), ("x", x, own2), ("y", y, tx1), ("c", c, tx1), ("c", c, tz1)],
    )
    r3, rx1, yx2, cx2, dx1 = stage(
        [], [("z", pairs(2, 4), in3), ("x", x, x_first), ("y", y, tx2), ("c", c, tx2), ("c", c, yx1)]
    )
    r4, tzx1, yz1, dx2 = stage(
        [], [("z", pairs(0, 6), wb), ("x", x, tz1), ("y", y, tz1), ("c", c, yx2)]
    )
    tz2, w4 = pick(r2, r3), pick(r3, r2)
    rx1_kv, rx1_q = rx1[:, :kv_width], rx1[:, kv_width:]
    part1 = spread(1, (tx1, yx1, cx1, dx1), (tx2, yx2, cx2, dx2))
    r5, z5, rx2, yzx1, dz1 = stage(
        [tz2, w4, rx1_kv, rx1_q],
        [("z", pairs(6, 0), rx1), ("z", both_ways, wb), ("x", x, x_second), ("y", y, tzx1), ("c", c, yz1)],
    )
    w6 = pick(r1, r4)
    near = part0 + part1
    n = len(near)
    acc_a = project(
        where, blocks(0, 4, 6), near, [(w, 0, n) for w in (wa, w4, w6)], depth, 0, width
    )
    r6, tzx2, yz2, czx1, dzx1 = stage(
        [acc_a],
        [("z", pairs(4, 2), rx2), ("x", x, tz2), ("y", y, tz2), ("c", c, tzx1), ("c", c, yzx1)],
    )
    rx2_kv, rx2_q = rx2[:, :kv_width], rx2[:, kv_width:]
    r5_q = r5[:, kv_width:]
    rxa = pick(rx2, rx1)
    five, w_five = [0, 4, 6, 1, 2], [wa, w4, w6, rxa, z5]
    six, last = blocks(*five, pick(3, 5)), blocks(pick(5, 3), 7)
    first2 = spread(2, (tz1, yz1, cz1, dz1), [None] * 4)[:4]
    acc_a = project(
        where, blocks(*five), near + first2,
        [(w, n, n + 4) for w in w_five[:3]] + [(w, 0, n + 4) for w in w_five[3:]], depth, 0, width,
        starts=[(acc_a, 0, 2 * rows, 0)],
    )
    r7, yzx2, cz2, czx2, dz2 = stage(
        [acc_a, rx2_kv, rx2_q, r5_q, six, last],
        [("z", pairs(2, 4), rx1_kv), ("y", y, tzx2), ("c", c, tz2), ("c", c, tzx2), ("c", c, yz2)],
        "all",
    )
    first3 = spread(3, (tzx1, yzx1, czx1, dzx1), [None] * 4)[:4]
    most = near + first2 + first3
    acc_b = project(
        where, six, most, [(w, n + 4, n + 8) for w in w_five] + [(r6, 0, n + 8)], depth, 0, width,
        starts=[(acc_a, 0, 2 * rows + rows // 2, 0)],
    )
    dzx2, r8 = stage([acc_b], [("c", c, yzx2), ("z", pairs(0, 6), rx2_kv)], "all")
    rest = spread(2, [None] * 4, (tz2, yz2, cz2, dz2))[4:]
    rest += spread(3, [None] * 4, (tzx2, yzx2, czx2, dzx2))[4:]
    acc_c = project(where, six, rest, [(w, 0, 8) for w in w_five + [r6]], depth, 0, width)
    r7q, r8q = stage(
        [acc_c], [("z", pairs(2, 4), rx1_q), ("z", pairs(0, 6), rx2_q)], ties=None
    )

    r8 = lax.optimization_barrier((r8, acc_c))[0]
    every = most + rest

    def finals(column):
        return [(acc_b, 0, 3 * rows, column), (acc_c, 0, rows, column)]

    keyval, tail, state = project(
        where, last, every, [(w, 0, len(every)) for w in (r7, (r8, r5))],
        depth, 0, kv_width, starts=finals(0), kind=(heads, size), ends=doc_ends,
    )
    other = hop(state, MEMBERS)
    queries = project(
        where, last, every, [(w, 0, len(every)) for w in (r7q, (r8q, r5_q))],
        depth, 0, q_width, starts=finals(q_block), kind="query",
    )

    outs, squares, sent = {}, 0.0, []
    for k in (3, 2, 1, 0):
        if k == 0:
            queries = lax.optimization_barrier((queries, sent[0]))[0]
        outs[k], square = attend(where, doc_ends, k, queries, keyval, tail, other)
        if k:
            outs[k], square = hop(outs[k], k), hop(square, k)
            sent.append(outs[k])
        squares = squares + square
    squares = squares + sum(side(squares, k) for k in range(1, fsdp_size))
    return finish(
        where, [outs[k] for k in range(MEMBERS)], squares, norm_gain[None, :],
        head_count * fsdp_size * size,
    )


def plain(tokens, w_query, w_keyval, doc_lengths, norm_gain):
    rows_here = tokens.shape[0]
    head_count = w_query.shape[1]
    head_size = w_query.shape[2]
    shard_index = lax.axis_index("seq")
    doc_ends = jnp.cumsum(doc_lengths)
    offsets = lax.iota(jnp.int32, rows_here)
    doc_ids = doc_index(shard_index * rows_here + offsets, doc_ends)
    first_doc = doc_ids[0]
    tail_doc = doc_ids[rows_here - 1]

    def project(panel_rows):
        panel = panel_rows.reshape(panel_rows.shape[0], panel_rows.shape[1] * panel_rows.shape[2])
        return jnp.dot(tokens, panel, preferred_element_type=jnp.float32)

    query_sum = project(lax.all_gather(w_query, "seq", axis=0, tiled=True))
    keyval_sum = project(lax.all_gather(w_keyval, "seq", axis=0, tiled=True))
    keyval = (
        jax.nn.silu(keyval_sum).astype(jnp.bfloat16).reshape(rows_here, head_count, 2 * head_size)
    )
    key_rows = keyval[:, :, :head_size]
    values = keyval[:, :, head_size:]
    tail_mask = (doc_ids == tail_doc).astype(jnp.bfloat16)
    tail_state = jnp.einsum(
        "thd,the->hde",
        key_rows * tail_mask[:, None, None],
        values,
        preferred_element_type=jnp.float32,
    )
    states = lax.all_gather(tail_state[None], "seq", axis=0, tiled=True)
    shard_ids = lax.iota(jnp.int32, states.shape[0])
    owner_docs = doc_index(shard_ids * rows_here + rows_here - 1, doc_ends)
    selected = ((shard_ids < shard_index) & (owner_docs == first_doc)).astype(jnp.float32)
    incoming = jnp.sum(selected[:, None, None, None] * states, axis=0)
    queries = jax.nn.silu(query_sum).astype(jnp.bfloat16).reshape(rows_here, head_count, head_size)
    scores = jnp.einsum("thd,shd->hts", queries, key_rows, preferred_element_type=jnp.float32)
    causal = (
        (offsets[:, None] >= offsets[None, :]) & (doc_ids[:, None] == doc_ids[None, :])
    ).astype(jnp.float32)
    weights = (scores * causal[None]).astype(jnp.bfloat16)
    within = jnp.einsum("hts,she->the", weights, values, preferred_element_type=jnp.float32)
    carried = jnp.einsum(
        "thd,hde->the", queries, incoming.astype(jnp.bfloat16), preferred_element_type=jnp.float32
    )
    carried = carried * (doc_ids == first_doc).astype(jnp.float32)[:, None, None]
    mixed = within + carried
    sum_squares = lax.psum(jnp.sum(mixed * mixed, axis=(1, 2)), "fsdp")
    inverse_rms = lax.rsqrt(sum_squares / (head_count * lax.axis_size("fsdp") * head_size) + 1e-06)
    flat = mixed.reshape(rows_here, head_count * head_size)
    return (flat * inverse_rms[:, None] * norm_gain.astype(jnp.float32)[None, :]).astype(
        jnp.bfloat16
    )


def solution(mesh):
    seq_size, fsdp_size = mesh.shape["seq"], mesh.shape["fsdp"]

    def body(tokens, w_query, *rest):
        rows, (depth, head_count, _) = tokens.shape[0], w_query.shape
        fits = seq_size == 2 * MEMBERS and fsdp_size == 4 and head_count % MEMBERS == 0
        if fits and rows == depth and rows % 128 == 0:
            return grouped(seq_size, fsdp_size, tokens, w_query, *rest)
        return plain(tokens, w_query, *rest)

    return jax.shard_map(
        body,
        mesh=mesh,
        in_specs=(P("seq", None), P("seq", "fsdp", None), P("seq", "fsdp", None), P(), P("fsdp")),
        out_specs=P("seq", "fsdp"),
        check_vma=False,
    )
```
